32 devices in a mesh: frame: 4 (over y, core), head: 4 (over z), fsdp: 2 (over x).
Axes of the slice: x: 2, y: 2, z: 4, core: 2. Of those that a mesh axis runs over, the one named last changes fastest.
Arguments:
- queries: bfloat16 [2, 8, 256, 5120], P('fsdp', 'frame', 'head'), may hold values from -6 to 6
- key_rows: bfloat16 [2, 8, 256, 5120], P('fsdp', 'frame', 'head'), may hold values from -6 to 6
- value_rows: bfloat16 [2, 8, 256, 5120], P('fsdp', 'frame', 'head'), may hold values from -6 to 6
- saved_out: bfloat16 [2, 8, 256, 5120], P('fsdp', 'frame', 'head'), may hold values from -6 to 6
- cotangent: bfloat16 [2, 8, 256, 5120], P('fsdp', 'frame', 'head'), may hold values from -192 to 192
- out_weight: bfloat16 [5120, 5120], P('head'), may hold values from -0.078125 to 0.078125
- gate_table: float32 [64, 5120], replicated, may hold values from 0.25 to 2.5
- levels: int32 [8], P('frame'), may hold values from 0 to 63, as said below
- reach_flags: int32 [8, 2], replicated, may hold values from 0 to 1
Outputs:
- d_queries: bfloat16 [2, 8, 256, 5120], P('fsdp', 'frame', None, 'head')
- d_keys: bfloat16 [2, 8, 256, 5120], P('fsdp', 'frame', None, 'head')
- d_values: bfloat16 [2, 8, 256, 5120], P('fsdp', 'frame', None, 'head')
- d_weight: float32 [5120, 5120], P('head', ('frame', 'fsdp'))
The draws below stay inside these ranges and needn't reach their ends.
Inputs may be any that keep to these rules, and one draw needn't show every extreme that they name: `levels`: each frame's level is at least the level of the frame before it; the first frame has level 0 and the last frame level 63.
All inputs are finite; a program needn't handle non-finite values.
Results may differ from the reference program's by a relative error of at most 0.017.
Values may be sent and summed in bfloat16 or wider, within the bound.
No kernel may reach another device: no remote copies, remote signals or barrier semaphores. Data moves between devices by JAX's collectives and lax.ppermute only.
A program may use at most 128 MiB of HBM per device.

```python
import math
from functools import reduce
import jax
import jax.numpy as jnp
from jax import lax

D = 5120
HD = 128
LEVELS = 64
FR_DEV = 2
TOKF = 256
FRAMES = 8
BATCH = 2


def draw_queries(key, part):
    own_key = jax.random.fold_in(key, 11)
    shape_all = (BATCH, FRAMES, TOKF, D)
    filled = jnp.clip(jax.random.normal(own_key, shape_all, jnp.float32), -6.0, 6.0)
    return filled.astype(jnp.bfloat16)


def draw_key_rows(key, part):
    own_key = jax.random.fold_in(key, 13)
    shape_all = (BATCH, FRAMES, TOKF, D)
    filled = jnp.clip(jax.random.normal(own_key, shape_all, jnp.float32), -6.0, 6.0)
    return filled.astype(jnp.bfloat16)


def draw_levels(key, part):
    increments = jax.random.randint(jax.random.fold_in(key, 23), (FRAMES,), 1, 5)
    increments = jnp.where(jnp.arange(FRAMES) == 0, 0, increments).astype(jnp.int32)
    running = jnp.cumsum(increments).astype(jnp.int32)
    return ((LEVELS - 1) * running // running[FRAMES - 1]).astype(jnp.int32)


def with_ends(result, stream_key, smallest, largest):
    longest = result.shape.index(max(result.shape))
    spots = []
    for shift in (0, 1):
        where = [jax.random.randint(jax.random.fold_in(stream_key, axis), (), 0, length) for axis, length in enumerate(result.shape)]
        where[longest] = (where[longest] + shift) % result.shape[longest]
        spots.append(tuple(where))
    return result.at[spots[0]].set(smallest).at[spots[1]].set(largest)


def raised(entries, stream_key, source, target, blocks, factor):
    owner, partner = [(jnp.arange(entries.shape[axis_at]) // (entries.shape[axis_at] // blocks)).reshape([-1 if axis == axis_at else 1 for axis in range(entries.ndim)]) for axis_at in (source, target)]
    chosen = jax.random.permutation(stream_key, blocks)[partner]
    strong = (owner == chosen) | (owner == (partner + blocks // 2) % blocks)
    return jnp.where(strong, factor * entries, entries)


def block_levels(rng, dims, cuts, smallest, largest):
    factor_of, own = 1.0, jax.random.fold_in(rng, 6)
    for axis_at, blocks in cuts:
        heights = jnp.exp(jax.random.uniform(jax.random.fold_in(own, axis_at), (blocks,), jnp.float32, smallest / len(cuts), largest / len(cuts)))
        factor_of = factor_of * jnp.repeat(heights, dims[axis_at] // blocks).reshape([-1 if axis == axis_at else 1 for axis in range(len(dims))])
    return factor_of


def bell_draw(stream_key, extent, deviation, reach, shards=(), held_as=jnp.bfloat16):
    values = jax.random.normal(stream_key, extent, jnp.float32) * deviation
    if len(shards) > 0:
        values = block_levels(stream_key, extent, shards, -0.22, 0.18) * values
    return jnp.clip(values, min=-reach, max=reach).astype(held_as)


def heavy_noise(key, dims, width, bound, cuts, heavy, held_as=jnp.bfloat16):
    result = width * jax.random.normal(key, dims, jnp.float32)
    if cuts:
        result = result * block_levels(key, dims, cuts, -0.22, 0.18)
    return jnp.clip(raised(result, jax.random.fold_in(key, 3), *heavy), -bound, bound).astype(held_as)


def setup_inputs(seed: int = 0) -> dict:
    key_of = jax.random.split(jax.random.key(seed), 10)
    return {
        "queries": draw_queries(jax.random.fold_in(key_of[9], 71), 0),
        "key_rows": draw_key_rows(jax.random.fold_in(key_of[9], 71), 0),
        "value_rows": bell_draw(key_of[2], (BATCH, FRAMES, TOKF, D), 1.0, 6.0, ((0, 2), (1, 4), (2, 4))),
        "saved_out": bell_draw(key_of[3], (BATCH, FRAMES, TOKF, D), 1.0, 6.0, ((0, 2), (1, 4), (2, 4))),
        "cotangent": heavy_noise(key_of[4], (BATCH, FRAMES, TOKF, D), 32.0, 192.0, ((0, 2), (1, 4), (2, 4)), (1, 3, 4, 2.0)),
        "out_weight": bell_draw(key_of[5], (D, D), D ** -0.5, 0.078125, ((0, 4),)),
        "gate_table": jnp.clip(jnp.exp(jax.random.uniform(key_of[6], (LEVELS, D), jnp.float32, math.log(0.25), math.log(2.5))), 0.25, 2.5),
        "levels": draw_levels(jax.random.fold_in(key_of[9], 71), 0),
        "reach_flags": with_ends(jax.random.randint(key_of[8], (FRAMES, 2), 0, 2), jax.random.fold_in(key_of[8], 1), 0, 1).astype(jnp.int32),
    }


NEG = -1e30


def block_scores(query_rows, key_block, inv_root):
    return jnp.einsum('thd,shd->hts', query_rows.astype(jnp.float32), key_block.astype(jnp.float32)) * inv_root


def row_stats(query_rows, key_list, allowed_set, inv_root):
    scores = [block_scores(query_rows, member, inv_root) for member in key_list]
    maxima = [jnp.max(jnp.where(allowed[None, None, :] > 0, score_block, NEG), axis=2) for score_block, allowed in zip(scores, allowed_set)]
    row_max = reduce(jnp.maximum, maxima)
    totals = [jnp.sum(jnp.where(allowed[None, None, :] > 0, jnp.exp(score_block - row_max[:, :, None]), 0.0), axis=2) for score_block, allowed in zip(scores, allowed_set)]
    return row_max + jnp.log(reduce(jnp.add, totals))


def block_grads(query_rows, d_out, key_block, value_block, log_total, row_delta, allowed, inv_root):
    scores = block_scores(query_rows, key_block, inv_root)
    prob_rows = jnp.where(allowed[None, None, :] > 0, jnp.exp(scores - log_total[:, :, None]), 0.0)
    probs_low = prob_rows.astype(jnp.bfloat16).astype(jnp.float32)
    d_wide = d_out.astype(jnp.float32)
    d_value = jnp.einsum('hts,thd->shd', probs_low, d_wide)
    d_probs = jnp.einsum('thd,shd->hts', d_wide, value_block.astype(jnp.float32))
    d_scores = (prob_rows * (d_probs - row_delta[:, :, None])).astype(jnp.bfloat16).astype(jnp.float32)
    d_query = jnp.einsum('hts,shd->thd', d_scores, key_block.astype(jnp.float32)) * inv_root
    d_key = jnp.einsum('hts,thd->shd', d_scores, query_rows.astype(jnp.float32)) * inv_root
    return d_query, d_key, d_value


def reach_mask(flag_value):
    half_count = TOKF // 2
    limit = half_count + (flag_value == 1).astype(jnp.int32) * (TOKF - half_count)
    return (jnp.arange(TOKF, dtype=jnp.int32) < limit).astype(jnp.float32)


def reference(queries, key_rows, value_rows, saved_out, cotangent, out_weight, gate_table, levels, reach_flags):
    inv_root = HD ** -0.5
    model_width = queries.shape[3]
    head_count = model_width // HD
    tokens_all = BATCH * FRAMES * TOKF
    choose = (levels[:, None] == jnp.arange(LEVELS, dtype=jnp.int32)[None, :]).astype(jnp.float32)
    frame_gain = jnp.dot(choose, gate_table, precision=lax.Precision.HIGHEST)
    gated = (cotangent.astype(jnp.float32) * frame_gain[None, :, None, :]).astype(jnp.bfloat16)
    d_low = jnp.einsum('bftd,ed->bfte', gated.astype(jnp.float32), out_weight.astype(jnp.float32)).astype(jnp.bfloat16)

    weight_grad = jnp.zeros((model_width, model_width), jnp.float32)
    for video in range(BATCH):
        for block_id in range(FRAMES // FR_DEV):
            first_frame = block_id * FR_DEV
            saved_rows = saved_out[video, first_frame:first_frame + FR_DEV].reshape(FR_DEV * TOKF, model_width)
            gated_rows = gated[video, first_frame:first_frame + FR_DEV].reshape(FR_DEV * TOKF, model_width)
            partial_sum = lax.dot_general(saved_rows, gated_rows, (((0,), (0,)), ((), ())), preferred_element_type=jnp.float32) / tokens_all
            rounded = lax.optimization_barrier(partial_sum.astype(jnp.bfloat16))
            weight_grad = weight_grad + rounded.astype(jnp.float32)

    def split_heads(array):
        return array.reshape(BATCH, FRAMES, TOKF, head_count, HD)

    q_five = split_heads(queries)
    k_five = split_heads(key_rows)
    v_five = split_heads(value_rows)
    o_five = split_heads(saved_out)
    d_five = split_heads(d_low)
    self_flag = jnp.ones((TOKF,), jnp.float32)
    video_q, video_k, video_v = [], [], []
    for video in range(BATCH):
        key_grads = [jnp.zeros((TOKF, head_count, HD), jnp.float32) for _ in range(FRAMES)]
        value_grads = [jnp.zeros((TOKF, head_count, HD), jnp.float32) for _ in range(FRAMES)]
        query_grads = []
        for frame_id in range(FRAMES):
            near_ids = []
            allowed_set = []
            for near_id in (frame_id - 1, frame_id, frame_id + 1):
                if 0 <= near_id < FRAMES:
                    near_ids.append(near_id)
                    if near_id == frame_id:
                        allowed_set.append(self_flag)
                    else:
                        column = 0 if near_id < frame_id else 1
                        allowed_set.append(reach_mask(reach_flags[frame_id, column]))
            query_rows = q_five[video, frame_id]
            log_total = row_stats(query_rows, [k_five[video, near_id] for near_id in near_ids], allowed_set, inv_root)
            row_delta = jnp.einsum('thd,thd->ht', d_five[video, frame_id].astype(jnp.float32), o_five[video, frame_id].astype(jnp.float32))
            query_grad = jnp.zeros((TOKF, head_count, HD), jnp.float32)
            for near_id, allowed in zip(near_ids, allowed_set):
                d_query, d_key, d_value = block_grads(query_rows, d_five[video, frame_id], k_five[video, near_id], v_five[video, near_id], log_total, row_delta, allowed, inv_root)
                query_grad = query_grad + d_query
                key_grads[near_id] = key_grads[near_id] + d_key
                value_grads[near_id] = value_grads[near_id] + d_value
            query_grads.append(query_grad)
        video_q.append(jnp.stack(query_grads))
        video_k.append(jnp.stack(key_grads))
        video_v.append(jnp.stack(value_grads))
    full_shape = (BATCH, FRAMES, TOKF, model_width)
    d_queries = jnp.stack(video_q).reshape(full_shape).astype(jnp.bfloat16)
    d_keys = jnp.stack(video_k).reshape(full_shape).astype(jnp.bfloat16)
    d_values = jnp.stack(video_v).reshape(full_shape).astype(jnp.bfloat16)
    return (d_queries, d_keys, d_values, weight_grad)
```

```python
from functools import partial

import jax
import jax.numpy as jnp
from jax import lax
from jax.experimental import pallas as pl
from jax.experimental.pallas import tpu as pltpu
from jax.sharding import PartitionSpec as P

HD = 128
NEG = -1e30
NT = (((1,), (1,)), ((), ()))
NN = (((1,), (0,)), ((), ()))
TN = (((0,), (0,)), ((), ()))


def dot(lhs, rhs, dims):
    return lax.dot_general(lhs, rhs, dims, preferred_element_type=jnp.float32)


def attention_kernel(
    limits, q_ref, k_ref, v_ref, o_ref, d_ref, kp_ref, kn_ref, vp_ref, vn_ref,
    dq_ref, dk_ref, dv_ref, dkp_ref, dkn_ref, dvp_ref, dvn_ref,
):
    frames = q_ref.shape[1]
    inv_root = HD ** (-0.5)

    def whole(ref, frame):
        return ref[:, frame].reshape(-1, HD)

    def side(ref):
        return ref[...].reshape(-1, HD)

    keys = [side(kp_ref)] + [whole(k_ref, f) for f in range(frames)] + [side(kn_ref)]
    vals = [side(vp_ref)] + [whole(v_ref, f) for f in range(frames)] + [side(vn_ref)]
    tokens = keys[0].shape[0]
    row = lax.broadcasted_iota(jnp.int32, (tokens, tokens), 0)
    key_grads = [None] * (frames + 2)
    value_grads = [None] * (frames + 2)

    def put(grads, slot, term):
        grads[slot] = term if grads[slot] is None else grads[slot] + term

    for f in range(frames):
        q, d = whole(q_ref, f), whole(d_ref, f)
        prod = d.astype(jnp.float32) * whole(o_ref, f).astype(jnp.float32)
        delta = lax.dot_general(
            jnp.ones((8, HD), jnp.float32), prod, NT,
            precision=lax.Precision.HIGHEST, preferred_element_type=jnp.float32,
        )[0:1]
        scores = []
        for w in range(3):
            s = dot(keys[f + w], q, NT) * inv_root
            if w != 1:
                s = jnp.where(row < limits[f, w // 2], s, NEG)
            scores.append(s)
        top = jnp.max(jnp.maximum(jnp.maximum(scores[0], scores[1]), scores[2]), axis=0, keepdims=True)
        exps = [jnp.exp(s - top) for s in scores]
        total = jnp.sum(exps[0] + exps[1] + exps[2], axis=0, keepdims=True)
        inv_total = 1.0 / total
        dq = None
        for w in range(3):
            prob = exps[w] * inv_total
            put(value_grads, f + w, dot(prob.astype(jnp.bfloat16), d, NN))
            d_prob = dot(vals[f + w], d, NT)
            d_score = (prob * (d_prob - delta)).astype(jnp.bfloat16)
            put(key_grads, f + w, dot(d_score, q, NN))
            term = dot(d_score, keys[f + w], TN)
            dq = term if dq is None else dq + term
        dq_ref[f] = (dq * inv_root).astype(jnp.bfloat16)
    for f in range(frames):
        dk_ref[f] = key_grads[f + 1] * inv_root
        dv_ref[f] = value_grads[f + 1]
    dkp_ref[...] = (key_grads[0] * inv_root).astype(jnp.bfloat16)
    dkn_ref[...] = (key_grads[frames + 1] * inv_root).astype(jnp.bfloat16)
    dvp_ref[...] = value_grads[0].astype(jnp.bfloat16)
    dvn_ref[...] = value_grads[frames + 1].astype(jnp.bfloat16)


def attention(limits, q, k, v, o, d, kp, kn, vp, vn):
    parts, frames, rows, width = q.shape
    tokens = parts * rows
    heads = width // HD
    whole = pl.BlockSpec((parts, frames, rows, HD), lambda h, lim: (0, 0, 0, h))
    side = pl.BlockSpec((parts, rows, HD), lambda h, lim: (0, 0, h))
    out = pl.BlockSpec((frames, tokens, HD), lambda h, lim: (0, 0, h))
    edge = pl.BlockSpec((tokens, HD), lambda h, lim: (0, h))
    full_shape, edge_shape = (frames, tokens, width), (tokens, width)
    return pl.pallas_call(
        attention_kernel,
        grid_spec=pltpu.PrefetchScalarGridSpec(
            num_scalar_prefetch=1,
            grid=(heads,),
            in_specs=[whole] * 5 + [side] * 4,
            out_specs=[out] * 3 + [edge] * 4,
        ),
        out_shape=[
            jax.ShapeDtypeStruct(full_shape, jnp.bfloat16),
            jax.ShapeDtypeStruct(full_shape, jnp.float32),
            jax.ShapeDtypeStruct(full_shape, jnp.float32),
        ]
        + [jax.ShapeDtypeStruct(edge_shape, jnp.bfloat16)] * 4,
        compiler_params=pltpu.CompilerParams(vmem_limit_bytes=48 * 2**20),
        cost_estimate=pl.CostEstimate(
            flops=heads * frames * 3 * tokens * tokens * HD * 10,
            bytes_accessed=heads * HD * tokens * frames * 2 * 16,
            transcendentals=heads * frames * 3 * tokens * tokens,
        ),
        name="attention_backward",
    )(limits, q, k, v, o, d, kp, kn, vp, vn)


def shifted(array, axis, step):
    count = lax.axis_size(axis)
    pairs = [(i, i + step) for i in range(count) if 0 <= i + step < count]
    return lax.ppermute(array, axis, pairs)


def per_device(
    queries, key_rows, value_rows, saved_out, cotangent, out_weight, gate_table, levels, reach_flags
):
    _, frames, rows, model = queries.shape
    parts = lax.axis_size("head")
    width = model // parts
    frames_all = frames * lax.axis_size("frame")
    tokens = rows * parts
    first_frame = lax.axis_index("frame") * frames
    tokens_all = lax.axis_size("fsdp") * frames_all * tokens

    gain = jnp.concatenate(
        [lax.dynamic_slice_in_dim(gate_table, levels[f], 1, axis=0) for f in range(frames)], axis=0
    )
    gated = (cotangent[0].astype(jnp.float32) * gain[:, None, :]).astype(jnp.bfloat16)
    gathered = lax.all_gather(gated, "head", axis=0, tiled=False)

    def exchange(array):
        split = jnp.stack([array[0, :, :, j * width : (j + 1) * width] for j in range(parts)])
        return lax.all_to_all(split, "head", split_axis=0, concat_axis=0, tiled=True)

    o, k, v, q = exchange(saved_out), exchange(key_rows), exchange(value_rows), exchange(queries)
    kp, kn = shifted(k[:, frames - 1], "frame", 1), shifted(k[:, 0], "frame", -1)
    vp, vn = shifted(v[:, frames - 1], "frame", 1), shifted(v[:, 0], "frame", -1)

    gated_rows = gathered.reshape(parts * frames * rows, model)
    d = dot(gated_rows, out_weight, NT).astype(jnp.bfloat16).reshape(parts, frames, rows, width)
    grad_t = dot(gated_rows, o.reshape(parts * frames * rows, width), TN)
    grad_t = (grad_t / tokens_all).astype(jnp.bfloat16)
    d_weight = lax.psum_scatter(
        grad_t, ("frame", "fsdp"), scatter_dimension=0, tiled=True
    ).T.astype(jnp.float32)

    ids = first_frame + jnp.arange(frames, dtype=jnp.int32)
    chosen = lax.dynamic_slice_in_dim(reach_flags, first_frame, frames, axis=0)
    inside = jnp.stack([ids > 0, ids < frames_all - 1], axis=1)
    limits = jnp.where(inside, jnp.where(chosen == 1, tokens, tokens // 2), 0).astype(jnp.int32)

    d_queries, dk, dv, dkp, dkn, dvp, dvn = attention(limits, q, k, v, o, d, kp, kn, vp, vn)

    def combine(own, to_prev, to_next):
        from_next = shifted(to_prev, "frame", -1)
        from_prev = shifted(to_next, "frame", 1)
        terms = [own[f] for f in range(frames)]
        terms[0] = terms[0] + from_prev.astype(jnp.float32)
        terms[frames - 1] = terms[frames - 1] + from_next.astype(jnp.float32)
        return jnp.stack(terms).astype(jnp.bfloat16)[None]

    return d_queries[None], combine(dk, dkp, dkn), combine(dv, dvp, dvn), d_weight


def solution(mesh):
    rows = P("fsdp", "frame", "head", None)
    heads = P("fsdp", "frame", None, "head")
    in_specs = (rows, rows, rows, rows, rows, P("head", None), P(), P("frame"), P())
    out_specs = (heads, heads, heads, P("head", ("frame", "fsdp")))
    return jax.shard_map(
        per_device, mesh=mesh, in_specs=in_specs, out_specs=out_specs, check_vma=False
    )
```

```python
from functools import partial

import jax
import jax.numpy as jnp
from jax import lax
from jax.experimental import pallas as pl
from jax.experimental.pallas import tpu as pltpu
from jax.sharding import PartitionSpec as P

HD = 128
NEG = -1e30
NT = (((1,), (1,)), ((), ()))
NN = (((1,), (0,)), ((), ()))
TN = (((0,), (0,)), ((), ()))


def dot(lhs, rhs, dims):
    return lax.dot_general(lhs, rhs, dims, preferred_element_type=jnp.float32)


def attention_kernel(parts, scal, *refs):
    own_q, own_k, own_v, own_o = refs[:4]
    packs = refs[4 : 4 + parts - 1]
    o_refs = refs[3 + parts : 2 + 2 * parts]
    d_ref, prev_ref, next_ref = refs[2 + 2 * parts : 5 + 2 * parts]
    dq_ref, dk_ref, dv_ref, to_prev_ref, to_next_ref = refs[5 + 2 * parts : 10 + 2 * parts]
    q_all, k_all, v_all, o_all, d_all = refs[10 + 2 * parts :]
    _, frames, rows, _ = own_q.shape
    me = scal[0]
    inv_root = HD ** (-0.5)
    for s in range(parts):
        source = lax.rem(me + parts - s, parts)
        at = pl.ds(pl.multiple_of(source * rows, rows), rows)
        for f in range(frames):
            q_all[f, at] = own_q[0, f] if s == 0 else packs[s - 1][2, f]
            k_all[f + 1, at] = own_k[0, f] if s == 0 else packs[s - 1][0, f]
            v_all[f + 1, at] = own_v[0, f] if s == 0 else packs[s - 1][1, f]
            o_all[f, at] = own_o[0, f] if s == 0 else o_refs[s - 1][f]
            d_all[f, at] = d_ref[s, f]
        k_all[0, at] = prev_ref[0, s]
        v_all[0, at] = prev_ref[1, s]
        k_all[frames + 1, at] = next_ref[0, s]
        v_all[frames + 1, at] = next_ref[1, s]
    tokens = rows * parts
    row = lax.broadcasted_iota(jnp.int32, (tokens, tokens), 0)
    key_grads = [None] * (frames + 2)
    value_grads = [None] * (frames + 2)

    def put(grads, slot, term):
        grads[slot] = term if grads[slot] is None else grads[slot] + term

    for f in range(frames):
        q, d = q_all[f], d_all[f]
        prod = d.astype(jnp.float32) * o_all[f].astype(jnp.float32)
        delta = lax.dot_general(
            jnp.ones((8, HD), jnp.float32), prod, NT,
            precision=lax.Precision.HIGHEST, preferred_element_type=jnp.float32,
        )[0:1]
        scores = []
        for w in range(3):
            s = dot(k_all[f + w], q, NT) * inv_root
            if w != 1:
                s = jnp.where(row < scal[2 + 2 * f + w // 2], s, NEG)
            scores.append(s)
        top = jnp.max(jnp.maximum(jnp.maximum(scores[0], scores[1]), scores[2]), axis=0, keepdims=True)
        exps = [jnp.exp(s - top) for s in scores]
        total = jnp.sum(exps[0] + exps[1] + exps[2], axis=0, keepdims=True)
        inv_total = 1.0 / total
        dq = None
        for w in range(3):
            prob = exps[w] * inv_total
            put(value_grads, f + w, dot(prob.astype(jnp.bfloat16), d, NN))
            d_prob = dot(v_all[f + w], d, NT)
            d_score = (prob * (d_prob - delta)).astype(jnp.bfloat16)
            put(key_grads, f + w, dot(d_score, q, NN))
            term = dot(d_score, k_all[f + w], TN)
            dq = term if dq is None else dq + term
        dq_ref[f] = (dq * inv_root).astype(jnp.bfloat16)
    for f in range(frames):
        dk_ref[f] = key_grads[f + 1] * inv_root
        dv_ref[f] = value_grads[f + 1]
    to_prev_ref[0] = (key_grads[0] * inv_root).astype(jnp.bfloat16)
    to_prev_ref[1] = value_grads[0].astype(jnp.bfloat16)
    to_next_ref[0] = (key_grads[frames + 1] * inv_root).astype(jnp.bfloat16)
    to_next_ref[1] = value_grads[frames + 1].astype(jnp.bfloat16)


def attention(scal, head0, heads, local, packs, o_pieces, d, from_prev, from_next):
    parts = len(packs) + 1
    _, frames, rows, _ = local[0].shape
    tokens, width = parts * rows, heads * HD
    own = pl.BlockSpec((1, frames, rows, HD), lambda h, sc: (0, 0, 0, sc[1] + head0 + h))
    pack = pl.BlockSpec((3, frames, rows, HD), lambda h, sc: (0, 0, 0, h))
    piece = pl.BlockSpec((frames, rows, HD), lambda h, sc: (0, 0, head0 + h))
    dsp = pl.BlockSpec((parts, frames, rows, HD), lambda h, sc: (0, 0, 0, head0 + h))
    halo = pl.BlockSpec((2, parts, rows, HD), lambda h, sc: (0, 0, 0, h))
    out = pl.BlockSpec((frames, tokens, HD), lambda h, sc: (0, 0, h))
    edge = pl.BlockSpec((2, tokens, HD), lambda h, sc: (0, 0, h))
    full_shape, edge_shape = (frames, tokens, width), (2, tokens, width)
    pads = pltpu.VMEM((frames + 2, tokens, HD), jnp.bfloat16)
    flats = pltpu.VMEM((frames, tokens, HD), jnp.bfloat16)
    return pl.pallas_call(
        partial(attention_kernel, parts),
        grid_spec=pltpu.PrefetchScalarGridSpec(
            num_scalar_prefetch=1,
            grid=(heads,),
            in_specs=[own] * 4 + [pack] * (parts - 1) + [piece] * (parts - 1) + [dsp, halo, halo],
            out_specs=[out] * 3 + [edge] * 2,
            scratch_shapes=[flats, pads, pads, flats, flats],
        ),
        out_shape=[
            jax.ShapeDtypeStruct(full_shape, jnp.bfloat16),
            jax.ShapeDtypeStruct(full_shape, jnp.float32),
            jax.ShapeDtypeStruct(full_shape, jnp.float32),
            jax.ShapeDtypeStruct(edge_shape, jnp.bfloat16),
            jax.ShapeDtypeStruct(edge_shape, jnp.bfloat16),
        ],
        compiler_params=pltpu.CompilerParams(vmem_limit_bytes=40 * 2**20),
        cost_estimate=pl.CostEstimate(
            flops=heads * frames * 3 * tokens * tokens * HD * 10,
            bytes_accessed=heads * HD * tokens * frames * 2 * 16,
            transcendentals=heads * frames * 3 * tokens * tokens,
        ),
        name="attention_backward",
    )(scal, *local, *packs, *o_pieces, d, from_prev, from_next)


def shifted(array, axis, step):
    count = lax.axis_size(axis)
    pairs = [(i, i + step) for i in range(count) if 0 <= i + step < count]
    return lax.ppermute(array, axis, pairs)


def rotated(array, axis, step):
    count = lax.axis_size(axis)
    return lax.ppermute(array, axis, [(i, (i + step) % count) for i in range(count)])


def after(array, event):
    return lax.optimization_barrier((array, event))


def line_step(right, left, axis, step):
    count = lax.axis_size(axis)
    right = lax.ppermute(right, axis, [(i, i + 1) for i in range(step - 1, count - 1)])
    left = lax.ppermute(left, axis, [(i, i - 1) for i in range(1, count - step + 1)])
    return right, left


def line_pieces(own, rights, lefts, axis):
    count, me = lax.axis_size(axis), lax.axis_index(axis)
    return [own] + [
        jnp.where(me >= r, rights[r - 1], lefts[count - r - 1]) for r in range(1, count)
    ]


def per_device(
    queries, key_rows, value_rows, saved_out, cotangent, out_weight, gate_table, levels, reach_flags
):
    _, frames, rows, model = queries.shape
    parts = lax.axis_size("head")
    me = lax.axis_index("head")
    width = model // parts
    heads = width // HD
    frames_all = frames * lax.axis_size("frame")
    tokens = rows * parts
    first_frame = lax.axis_index("frame") * frames
    tokens_all = lax.axis_size("fsdp") * frames_all * tokens
    blocks = lax.axis_size("frame") * lax.axis_size("fsdp")
    block = model // blocks
    cut = (block // 2) // 128 * 128 or block // 2

    def columns_for(array, step, start, size):
        target = lax.rem(me + step, parts)
        return lax.dynamic_slice_in_dim(array[0], target * width + start, size, axis=2)

    o_pieces = [
        rotated(columns_for(saved_out, s, 0, width), "head", s) for s in range(1, parts)
    ]

    gain = jnp.concatenate(
        [lax.dynamic_slice_in_dim(gate_table, levels[f], 1, axis=0) for f in range(frames)], axis=0
    )
    gated = (cotangent[0].astype(jnp.float32) * gain[:, None, :]).astype(jnp.bfloat16)
    gated = gated.reshape(frames * rows, model)
    rest = block - cut
    chunk0 = jnp.concatenate([gated[:, b * block :][:, :cut] for b in range(blocks)], axis=1)
    chunk1 = jnp.concatenate([gated[:, b * block + cut :][:, :rest] for b in range(blocks)], axis=1)

    rights, lefts = [[], []], [[], []]
    right, left = chunk0, chunk0
    for step in range(1, parts):
        right, left = line_step(right, left, "head", step)
        if step == 1:
            chunk1, right = after(chunk1, right)
        rights[0].append(right)
        lefts[0].append(left)
    right, left = chunk1, chunk1
    for step in range(1, parts):
        right, left = line_step(right, left, "head", step)
        rights[1].append(right)
        lefts[1].append(left)

    def weight_chunk(pieces, o_rows):
        rows_c = jnp.concatenate(pieces, axis=0)
        grad = dot(rows_c, o_rows, TN)
        grad = (grad / tokens_all).astype(jnp.bfloat16)
        return rows_c, lax.psum_scatter(grad, ("frame", "fsdp"), scatter_dimension=0, tiled=True)

    own_o = columns_for(saved_out, 0, 0, width)
    o_rows = jnp.concatenate(
        [piece.reshape(frames * rows, width) for piece in [own_o] + o_pieces], axis=0
    )
    rows0, grad0 = weight_chunk(line_pieces(chunk0, rights[0], lefts[0], "head"), o_rows)
    rows1, grad1 = weight_chunk(line_pieces(chunk1, rights[1], lefts[1], "head"), o_rows)
    d_weight = jnp.concatenate([grad0, grad1], axis=0).T.astype(jnp.float32)

    columns = []
    for b in range(blocks):
        columns += [rows0[:, b * cut : (b + 1) * cut], rows1[:, b * rest : (b + 1) * rest]]
    gated_rows = jnp.concatenate(columns, axis=1)
    d = dot(gated_rows, out_weight, NT).astype(jnp.bfloat16).reshape(parts, frames, rows, width)

    ids = first_frame + jnp.arange(frames, dtype=jnp.int32)
    chosen = lax.dynamic_slice_in_dim(reach_flags, first_frame, frames, axis=0)
    inside = jnp.stack([ids > 0, ids < frames_all - 1], axis=1)
    limits = jnp.where(inside, jnp.where(chosen == 1, tokens, tokens // 2), 0).astype(jnp.int32)
    scal = jnp.concatenate([jnp.stack([me, me * heads]).astype(jnp.int32), limits.reshape(-1)])

    first = (heads + 1) // 2
    groups = [(0, first), (first, heads - first)]
    results = []
    for g, (head0, count) in enumerate(groups):
        start, size = head0 * HD, count * HD

        def packed(step):
            return jnp.stack(
                [columns_for(a, step, start, size) for a in (key_rows, value_rows, queries)]
            )

        packs = [packed(s) for s in range(1, parts)]
        event = rights[g][parts - 2]
        packs, event = after(packs, event)
        rights[g][parts - 2] = event
        packs = [rotated(p, "head", s) for s, p in zip(range(1, parts), packs)]
        own = [columns_for(a, 0, start, size) for a in (key_rows, value_rows)]

        def boundary(frame):
            return jnp.stack(
                [jnp.stack([own[t][frame]] + [p[t, frame] for p in packs]) for t in range(2)]
            )

        from_prev = shifted(boundary(frames - 1), "frame", 1)
        from_next = shifted(boundary(0), "frame", -1)
        local = (queries, key_rows, value_rows, saved_out)
        dq, dk, dv, to_prev, to_next = attention(
            scal, head0, count, local, packs, o_pieces, d, from_prev, from_next
        )
        grad_next = shifted(to_prev, "frame", -1)
        grad_prev = shifted(to_next, "frame", 1)

        def combine(own_grad, t):
            terms = [own_grad[f] for f in range(frames)]
            terms[0] = terms[0] + grad_prev[t].astype(jnp.float32)
            terms[frames - 1] = terms[frames - 1] + grad_next[t].astype(jnp.float32)
            return jnp.stack(terms).astype(jnp.bfloat16)

        results.append((dq, combine(dk, 0), combine(dv, 1)))

    d_queries, d_keys, d_values = (
        jnp.concatenate([r[i] for r in results], axis=2)[None] for i in range(3)
    )
    return d_queries, d_keys, d_values, d_weight


def solution(mesh):
    rows = P("fsdp", "frame", "head", None)
    heads = P("fsdp", "frame", None, "head")
    in_specs = (rows, rows, rows, rows, rows, P("head", None), P(), P("frame"), P())
    out_specs = (heads, heads, heads, P("head", ("frame", "fsdp")))
    return jax.shard_map(
        per_device, mesh=mesh, in_specs=in_specs, out_specs=out_specs, check_vma=False
    )
```

```python
from functools import partial

import jax
import jax.numpy as jnp
from jax import lax
from jax.experimental import pallas as pl
from jax.experimental.pallas import tpu as pltpu
from jax.sharding import PartitionSpec as P

HD = 128
NEG = -1e30
NT = (((1,), (1,)), ((), ()))
NN = (((1,), (0,)), ((), ()))
TN = (((0,), (0,)), ((), ()))


def dot(lhs, rhs, dims):
    return lax.dot_general(lhs, rhs, dims, preferred_element_type=jnp.float32)


def attention_kernel(parts, scal, *refs):
    own_q, own_k, own_v, own_o = refs[:4]
    others, refs = parts - 1, refs[4:]
    kv_refs, q_refs, o_refs = refs[:others], refs[others : 2 * others], refs[2 * others : 3 * others]
    d_ref, prev_ref, next_ref, dq_ref, dk_ref, dv_ref, to_prev_ref, to_next_ref = refs[
        3 * others : 3 * others + 8
    ]
    q_all, k_all, v_all, o_all, d_all = refs[3 * others + 8 :]
    _, frames, rows, _ = own_q.shape
    me = scal[0]
    inv_root = HD ** (-0.5)
    for s in range(parts):
        source = lax.rem(me + parts - s, parts)
        at = pl.ds(pl.multiple_of(source * rows, rows), rows)
        for f in range(frames):
            q_all[f, at] = own_q[0, f] if s == 0 else q_refs[s - 1][f]
            k_all[f + 1, at] = own_k[0, f] if s == 0 else kv_refs[s - 1][0, f]
            v_all[f + 1, at] = own_v[0, f] if s == 0 else kv_refs[s - 1][1, f]
            o_all[f, at] = own_o[0, f] if s == 0 else o_refs[s - 1][f]
            d_all[f, at] = d_ref[s, f]
        k_all[0, at] = prev_ref[0, s]
        v_all[0, at] = prev_ref[1, s]
        k_all[frames + 1, at] = next_ref[0, s]
        v_all[frames + 1, at] = next_ref[1, s]
    tokens = rows * parts
    row = lax.broadcasted_iota(jnp.int32, (tokens, tokens), 0)
    key_grads = [None] * (frames + 2)
    value_grads = [None] * (frames + 2)

    def put(grads, slot, term):
        grads[slot] = term if grads[slot] is None else grads[slot] + term

    for f in range(frames):
        q, d = q_all[f], d_all[f]
        prod = d.astype(jnp.float32) * o_all[f].astype(jnp.float32)
        delta = lax.dot_general(
            jnp.ones((8, HD), jnp.float32), prod, NT,
            precision=lax.Precision.HIGHEST, preferred_element_type=jnp.float32,
        )[0:1]
        scores = []
        for w in range(3):
            s = dot(k_all[f + w], q, NT) * inv_root
            if w != 1:
                s = jnp.where(row < scal[2 + 2 * f + w // 2], s, NEG)
            scores.append(s)
        top = jnp.max(jnp.maximum(jnp.maximum(scores[0], scores[1]), scores[2]), axis=0, keepdims=True)
        exps = [jnp.exp(s - top) for s in scores]
        total = jnp.sum(exps[0] + exps[1] + exps[2], axis=0, keepdims=True)
        inv_total = 1.0 / total
        dq = None
        for w in range(3):
            prob = exps[w] * inv_total
            put(value_grads, f + w, dot(prob.astype(jnp.bfloat16), d, NN))
            d_prob = dot(v_all[f + w], d, NT)
            d_score = (prob * (d_prob - delta)).astype(jnp.bfloat16)
            put(key_grads, f + w, dot(d_score, q, NN))
            term = dot(d_score, k_all[f + w], TN)
            dq = term if dq is None else dq + term
        dq_ref[f] = (dq * inv_root).astype(jnp.bfloat16)
    for f in range(frames):
        dk_ref[f] = key_grads[f + 1] * inv_root
        dv_ref[f] = value_grads[f + 1]
    to_prev_ref[0] = (key_grads[0] * inv_root).astype(jnp.bfloat16)
    to_prev_ref[1] = value_grads[0].astype(jnp.bfloat16)
    to_next_ref[0] = (key_grads[frames + 1] * inv_root).astype(jnp.bfloat16)
    to_next_ref[1] = value_grads[frames + 1].astype(jnp.bfloat16)


def attention(scal, head0, heads, local, kv, q_pieces, o_pieces, d, from_prev, from_next):
    parts = len(kv) + 1
    _, frames, rows, _ = local[0].shape
    tokens, width = parts * rows, heads * HD
    own = pl.BlockSpec((1, frames, rows, HD), lambda h, sc: (0, 0, 0, sc[1] + head0 + h))
    pack = pl.BlockSpec((2, frames, rows, HD), lambda h, sc: (0, 0, 0, head0 + h))
    q_spec = pl.BlockSpec((frames, rows, HD), lambda h, sc: (0, 0, h))
    piece = pl.BlockSpec((frames, rows, HD), lambda h, sc: (0, 0, head0 + h))
    dsp = pl.BlockSpec((parts, frames, rows, HD), lambda h, sc: (0, 0, 0, head0 + h))
    halo = pl.BlockSpec((2, parts, rows, HD), lambda h, sc: (0, 0, 0, head0 + h))
    out = pl.BlockSpec((frames, tokens, HD), lambda h, sc: (0, 0, h))
    edge = pl.BlockSpec((2, tokens, HD), lambda h, sc: (0, 0, h))
    full_shape, edge_shape = (frames, tokens, width), (2, tokens, width)
    pads = pltpu.VMEM((frames + 2, tokens, HD), jnp.bfloat16)
    flats = pltpu.VMEM((frames, tokens, HD), jnp.bfloat16)
    return pl.pallas_call(
        partial(attention_kernel, parts),
        grid_spec=pltpu.PrefetchScalarGridSpec(
            num_scalar_prefetch=1,
            grid=(heads,),
            in_specs=[own] * 4
            + [pack] * (parts - 1)
            + [q_spec] * (parts - 1)
            + [piece] * (parts - 1)
            + [dsp, halo, halo],
            out_specs=[out] * 3 + [edge] * 2,
            scratch_shapes=[flats, pads, pads, flats, flats],
        ),
        out_shape=[
            jax.ShapeDtypeStruct(full_shape, jnp.bfloat16),
            jax.ShapeDtypeStruct(full_shape, jnp.float32),
            jax.ShapeDtypeStruct(full_shape, jnp.float32),
            jax.ShapeDtypeStruct(edge_shape, jnp.bfloat16),
            jax.ShapeDtypeStruct(edge_shape, jnp.bfloat16),
        ],
        compiler_params=pltpu.CompilerParams(vmem_limit_bytes=40 * 2**20),
        cost_estimate=pl.CostEstimate(
            flops=heads * frames * 3 * tokens * tokens * HD * 10,
            bytes_accessed=heads * HD * tokens * frames * 2 * 16,
            transcendentals=heads * frames * 3 * tokens * tokens,
        ),
        name="attention_backward",
    )(scal, *local, *kv, *q_pieces, *o_pieces, d, from_prev, from_next)


def shifted(array, axis, step):
    count = lax.axis_size(axis)
    pairs = [(i, i + step) for i in range(count) if 0 <= i + step < count]
    return lax.ppermute(array, axis, pairs)


def rotated(array, axis, step):
    count = lax.axis_size(axis)
    return lax.ppermute(array, axis, [(i, (i + step) % count) for i in range(count)])


def after(array, event):
    return lax.optimization_barrier((array, event))


def line_step(right, left, axis, step):
    count = lax.axis_size(axis)
    right = lax.ppermute(right, axis, [(i, i + 1) for i in range(step - 1, count - 1)])
    left = lax.ppermute(left, axis, [(i, i - 1) for i in range(1, count - step + 1)])
    return right, left


def line_pieces(own, rights, lefts, axis):
    count, me = lax.axis_size(axis), lax.axis_index(axis)
    return [own] + [
        jnp.where(me >= r, rights[r - 1], lefts[count - r - 1]) for r in range(1, count)
    ]


def per_device(
    queries, key_rows, value_rows, saved_out, cotangent, out_weight, gate_table, levels, reach_flags
):
    _, frames, rows, model = queries.shape
    parts = lax.axis_size("head")
    me = lax.axis_index("head")
    width = model // parts
    heads = width // HD
    frames_all = frames * lax.axis_size("frame")
    tokens = rows * parts
    first_frame = lax.axis_index("frame") * frames
    tokens_all = lax.axis_size("fsdp") * frames_all * tokens
    blocks = lax.axis_size("frame") * lax.axis_size("fsdp")
    block = model // blocks
    cut = (block // 2) // 128 * 128 or block // 2

    def columns_for(array, step, start, size):
        target = lax.rem(me + step, parts)
        return lax.dynamic_slice_in_dim(array[0], target * width + start, size, axis=2)

    shifts = range(1, parts)
    o_pieces = [rotated(columns_for(saved_out, s, 0, width), "head", s) for s in shifts]

    gain = jnp.concatenate(
        [lax.dynamic_slice_in_dim(gate_table, levels[f], 1, axis=0) for f in range(frames)], axis=0
    )
    gated = (cotangent[0].astype(jnp.float32) * gain[:, None, :]).astype(jnp.bfloat16)
    gated = gated.reshape(frames * rows, model)
    rest = block - cut
    chunk0 = jnp.concatenate([gated[:, b * block :][:, :cut] for b in range(blocks)], axis=1)
    chunk1 = jnp.concatenate([gated[:, b * block + cut :][:, :rest] for b in range(blocks)], axis=1)

    ways = [[(chunk0, chunk0)], [(chunk1, chunk1)]]
    for step in shifts:
        if step == 2:
            o_pieces, ways[1][-1] = after(o_pieces, ways[1][-1])
        if step == parts - 1:
            ways[0][-1], ways[1][1] = after(ways[0][-1], ways[1][1])
        ways[0].append(line_step(*ways[0][-1], "head", step))
        if step < parts - 1:
            ways[1].append(line_step(*ways[1][-1], "head", step))
    kv_send = [
        jnp.stack([columns_for(a, s, 0, width) for a in (key_rows, value_rows)]) for s in shifts
    ]
    ways[0][-1], ways[1][-1] = after(ways[0][-1], ways[1][-1])
    kv_send, ways[0][-1] = after(kv_send, ways[0][-1])
    kv = [rotated(a, "head", s) for s, a in zip(shifts, kv_send)]
    ways[1].append(line_step(*ways[1][-1], "head", parts - 1))

    first = (heads + 1) // 2
    groups = [(0, first), (first, heads - first)]
    q_send = [
        [columns_for(queries, s, head0 * HD, count * HD) for s in shifts]
        for head0, count in groups
    ]
    q_send, ways[1][-1] = after(q_send, ways[1][-1])
    q_pieces = [[rotated(a, "head", s) for s, a in zip(shifts, sends)] for sends in q_send]

    def pieces(own, way):
        return line_pieces(own, [w[0] for w in way[1:]], [w[1] for w in way[1:]], "head")

    def weight_chunk(rows_c, o_rows):
        grad = dot(rows_c, o_rows, TN)
        grad = (grad / tokens_all).astype(jnp.bfloat16)
        return lax.psum_scatter(grad, ("frame", "fsdp"), scatter_dimension=0, tiled=True)

    own_o = columns_for(saved_out, 0, 0, width)
    o_rows = jnp.concatenate(
        [piece.reshape(frames * rows, width) for piece in [own_o] + o_pieces], axis=0
    )
    rows0 = jnp.concatenate(pieces(chunk0, ways[0]), axis=0)
    rows1 = jnp.concatenate(pieces(chunk1, ways[1]), axis=0)
    grad0 = weight_chunk(rows0, o_rows)
    grad1 = weight_chunk(rows1, o_rows)
    d_weight = jnp.concatenate([grad0, grad1], axis=0).T.astype(jnp.float32)

    columns = []
    for b in range(blocks):
        columns += [rows0[:, b * cut : (b + 1) * cut], rows1[:, b * rest : (b + 1) * rest]]
    gated_rows = jnp.concatenate(columns, axis=1)
    d = dot(gated_rows, out_weight, NT).astype(jnp.bfloat16).reshape(parts, frames, rows, width)

    ids = first_frame + jnp.arange(frames, dtype=jnp.int32)
    chosen = lax.dynamic_slice_in_dim(reach_flags, first_frame, frames, axis=0)
    inside = jnp.stack([ids > 0, ids < frames_all - 1], axis=1)
    limits = jnp.where(inside, jnp.where(chosen == 1, tokens, tokens // 2), 0).astype(jnp.int32)
    scal = jnp.concatenate([jnp.stack([me, me * heads]).astype(jnp.int32), limits.reshape(-1)])

    kv, d = after(kv, d)
    own = [columns_for(a, 0, 0, width) for a in (key_rows, value_rows)]

    def boundary(frame):
        return jnp.stack(
            [jnp.stack([own[t][frame]] + [p[t, frame] for p in kv]) for t in range(2)]
        )

    from_prev = shifted(boundary(frames - 1), "frame", 1)
    from_next = shifted(boundary(0), "frame", -1)
    local = (queries, key_rows, value_rows, saved_out)
    results = []
    for (head0, count), q_group in zip(groups, q_pieces):
        if results:
            q_group, results[-1][0] = after(q_group, results[-1][0])
        dq, dk, dv, to_prev, to_next = attention(
            scal, head0, count, local, kv, q_group, o_pieces, d, from_prev, from_next
        )
        grad_next = shifted(to_prev, "frame", -1)
        grad_prev = shifted(to_next, "frame", 1)
        results.append([dq, dk, dv, grad_prev, grad_next])

    def combine(own_grad, t, grad_prev, grad_next):
        terms = [own_grad[f] for f in range(frames)]
        terms[0] = terms[0] + grad_prev[t].astype(jnp.float32)
        terms[frames - 1] = terms[frames - 1] + grad_next[t].astype(jnp.float32)
        return jnp.stack(terms).astype(jnp.bfloat16)

    d_queries = jnp.concatenate([r[0] for r in results], axis=2)[None]
    d_keys = jnp.concatenate([combine(r[1], 0, r[3], r[4]) for r in results], axis=2)[None]
    d_values = jnp.concatenate([combine(r[2], 1, r[3], r[4]) for r in results], axis=2)[None]
    return d_queries, d_keys, d_values, d_weight


def solution(mesh):
    rows = P("fsdp", "frame", "head", None)
    heads = P("fsdp", "frame", None, "head")
    in_specs = (rows, rows, rows, rows, rows, P("head", None), P(), P("frame"), P())
    out_specs = (heads, heads, heads, P("head", ("frame", "fsdp")))
    return jax.shard_map(
        per_device, mesh=mesh, in_specs=in_specs, out_specs=out_specs, check_vma=False
    )
```

```python
from functools import partial

import jax
import jax.numpy as jnp
from jax import lax
from jax.experimental import pallas as pl
from jax.experimental.pallas import tpu as pltpu
from jax.sharding import PartitionSpec as P

HD = 128
NEG = -1e30
NT = (((1,), (1,)), ((), ()))
NN = (((1,), (0,)), ((), ()))
TN = (((0,), (0,)), ((), ()))


def dot(lhs, rhs, dims):
    return lax.dot_general(lhs, rhs, dims, preferred_element_type=jnp.float32)


def attention_kernel(parts, scal, *refs):
    own_q, own_k, own_v = refs[:3]
    others, refs = parts - 1, refs[3:]
    kv_refs, q_refs, refs = refs[:others], refs[others : 2 * others], refs[2 * others :]
    o_ref, d_ref, prev_ref, next_ref, dq_ref, dk_ref, dv_ref, to_prev_ref, to_next_ref = refs[:9]
    q_all, k_all, v_all = refs[9:]
    _, frames, rows, _ = own_q.shape
    me = scal[0]
    inv_root = HD ** (-0.5)
    for s in range(parts):
        source = lax.rem(me + parts - s, parts)
        at = pl.ds(pl.multiple_of(source * rows, rows), rows)
        for f in range(frames):
            q_all[f, at] = own_q[0, f] if s == 0 else q_refs[s - 1][f]
            k_all[f + 1, at] = own_k[0, f] if s == 0 else kv_refs[s - 1][0, f]
            v_all[f + 1, at] = own_v[0, f] if s == 0 else kv_refs[s - 1][1, f]
        k_all[0, at] = prev_ref[0, s]
        v_all[0, at] = prev_ref[1, s]
        k_all[frames + 1, at] = next_ref[0, s]
        v_all[frames + 1, at] = next_ref[1, s]
    tokens = rows * parts
    row = lax.broadcasted_iota(jnp.int32, (tokens, tokens), 0)
    key_grads = [None] * (frames + 2)
    value_grads = [None] * (frames + 2)

    def put(grads, slot, term):
        grads[slot] = term if grads[slot] is None else grads[slot] + term

    for f in range(frames):
        q, d = q_all[f], d_ref[:, f].reshape(tokens, HD)
        prod = d.astype(jnp.float32) * o_ref[:, f].reshape(tokens, HD).astype(jnp.float32)
        delta = lax.dot_general(
            jnp.ones((8, HD), jnp.float32), prod, NT,
            precision=lax.Precision.HIGHEST, preferred_element_type=jnp.float32,
        )[0:1]
        scores = []
        for w in range(3):
            s = dot(k_all[f + w], q, NT) * inv_root
            if w != 1:
                s = jnp.where(row < scal[2 + 2 * f + w // 2], s, NEG)
            scores.append(s)
        top = jnp.max(jnp.maximum(jnp.maximum(scores[0], scores[1]), scores[2]), axis=0, keepdims=True)
        exps = [jnp.exp(s - top) for s in scores]
        total = jnp.sum(exps[0] + exps[1] + exps[2], axis=0, keepdims=True)
        inv_total = 1.0 / total
        dq = None
        for w in range(3):
            prob = exps[w] * inv_total
            put(value_grads, f + w, dot(prob.astype(jnp.bfloat16), d, NN))
            d_prob = dot(v_all[f + w], d, NT)
            d_score = (prob * (d_prob - delta)).astype(jnp.bfloat16)
            put(key_grads, f + w, dot(d_score, q, NN))
            term = dot(d_score, k_all[f + w], TN)
            dq = term if dq is None else dq + term
        dq_ref[f] = (dq * inv_root).astype(jnp.bfloat16)
    for f in range(frames):
        dk_ref[f] = key_grads[f + 1] * inv_root
        dv_ref[f] = value_grads[f + 1]
    to_prev_ref[0] = (key_grads[0] * inv_root).astype(jnp.bfloat16)
    to_prev_ref[1] = value_grads[0].astype(jnp.bfloat16)
    to_next_ref[0] = (key_grads[frames + 1] * inv_root).astype(jnp.bfloat16)
    to_next_ref[1] = value_grads[frames + 1].astype(jnp.bfloat16)


def attention(scal, head0, heads, local, kv, q_pieces, o, d, from_prev, from_next):
    parts = len(kv) + 1
    _, frames, rows, _ = local[0].shape
    tokens, width = parts * rows, heads * HD
    own = pl.BlockSpec((1, frames, rows, HD), lambda h, sc: (0, 0, 0, sc[1] + head0 + h))
    pack = pl.BlockSpec((2, frames, rows, HD), lambda h, sc: (0, 0, 0, head0 + h))
    q_spec = pl.BlockSpec((frames, rows, HD), lambda h, sc: (0, 0, h))
    dsp = pl.BlockSpec((parts, frames, rows, HD), lambda h, sc: (0, 0, 0, head0 + h))
    halo = pl.BlockSpec((2, parts, rows, HD), lambda h, sc: (0, 0, 0, head0 + h))
    out = pl.BlockSpec((frames, tokens, HD), lambda h, sc: (0, 0, h))
    edge = pl.BlockSpec((2, tokens, HD), lambda h, sc: (0, 0, h))
    full_shape, edge_shape = (frames, tokens, width), (2, tokens, width)
    pads = pltpu.VMEM((frames + 2, tokens, HD), jnp.bfloat16)
    flats = pltpu.VMEM((frames, tokens, HD), jnp.bfloat16)
    return pl.pallas_call(
        partial(attention_kernel, parts),
        grid_spec=pltpu.PrefetchScalarGridSpec(
            num_scalar_prefetch=1,
            grid=(heads,),
            in_specs=[own] * 3
            + [pack] * (parts - 1)
            + [q_spec] * (parts - 1)
            + [dsp, dsp, halo, halo],
            out_specs=[out] * 3 + [edge] * 2,
            scratch_shapes=[flats, pads, pads],
        ),
        out_shape=[
            jax.ShapeDtypeStruct(full_shape, jnp.bfloat16),
            jax.ShapeDtypeStruct(full_shape, jnp.float32),
            jax.ShapeDtypeStruct(full_shape, jnp.float32),
            jax.ShapeDtypeStruct(edge_shape, jnp.bfloat16),
            jax.ShapeDtypeStruct(edge_shape, jnp.bfloat16),
        ],
        compiler_params=pltpu.CompilerParams(vmem_limit_bytes=40 * 2**20),
        cost_estimate=pl.CostEstimate(
            flops=heads * frames * 3 * tokens * tokens * HD * 10,
            bytes_accessed=heads * HD * tokens * frames * 2 * 16,
            transcendentals=heads * frames * 3 * tokens * tokens,
        ),
        name="attention_backward",
    )(scal, *local, *kv, *q_pieces, o, d, from_prev, from_next)


def shifted(array, axis, step):
    count = lax.axis_size(axis)
    pairs = [(i, i + step) for i in range(count) if 0 <= i + step < count]
    return lax.ppermute(array, axis, pairs)


def rotated(array, axis, step):
    count = lax.axis_size(axis)
    return lax.ppermute(array, axis, [(i, (i + step) % count) for i in range(count)])


def after(array, event):
    return lax.optimization_barrier((array, event))


def flipped(array, axis, bit):
    return lax.ppermute(array, axis, [(i, i ^ bit) for i in range(lax.axis_size(axis))])


def weight_kernel(scale, table, near_ref, far_ref, g_near, g_far, out_ref):
    step = pl.program_id(0)

    @pl.when(step == 0)
    def _():
        out_ref[...] = jnp.zeros_like(out_ref)

    total = dot(near_ref[0], g_near[0], TN) + dot(far_ref[0], g_far[0], TN)
    out_ref[...] += total * scale


def weight_grad(table, near, far, gated, scale):
    count, rows, width = near.shape
    columns = gated.shape[2]
    side = pl.BlockSpec((1, rows, width), lambda j, tab: (j, 0, 0))
    return pl.pallas_call(
        partial(weight_kernel, scale),
        grid_spec=pltpu.PrefetchScalarGridSpec(
            num_scalar_prefetch=1,
            grid=(count,),
            in_specs=[
                side,
                side,
                pl.BlockSpec((1, rows, columns), lambda j, tab: (tab[0, j], 0, 0)),
                pl.BlockSpec((1, rows, columns), lambda j, tab: (tab[1, j], 0, 0)),
            ],
            out_specs=pl.BlockSpec((width, columns), lambda j, tab: (0, 0)),
        ),
        out_shape=jax.ShapeDtypeStruct((width, columns), jnp.float32),
        compiler_params=pltpu.CompilerParams(vmem_limit_bytes=40 * 2**20),
        cost_estimate=pl.CostEstimate(
            flops=4 * count * rows * width * columns,
            bytes_accessed=4 * count * rows * (width + columns) + 4 * width * columns,
            transcendentals=0,
        ),
        name="weight_gradient",
    )(table, near, far, gated, gated)


def per_device(
    queries, key_rows, value_rows, saved_out, cotangent, out_weight, gate_table, levels, reach_flags
):
    _, frames, rows, model = queries.shape
    parts = lax.axis_size("head")
    me = lax.axis_index("head")
    width = model // parts
    heads = width // HD
    frames_all = frames * lax.axis_size("frame")
    tokens = rows * parts
    first_frame = lax.axis_index("frame") * frames
    tokens_all = lax.axis_size("fsdp") * frames_all * tokens
    blocks = lax.axis_size("frame") * lax.axis_size("fsdp")
    block = model // blocks
    def columns_for(array, step, start, size):
        target = lax.rem(me + step, parts)
        return lax.dynamic_slice_in_dim(array[0], target * width + start, size, axis=2)

    shifts = range(1, parts)
    shifts = range(1, parts)
    o_pieces = [rotated(columns_for(saved_out, s, 0, width), "head", s) for s in shifts]

    gain = jnp.concatenate(
        [lax.dynamic_slice_in_dim(gate_table, levels[f], 1, axis=0) for f in range(frames)], axis=0
    )
    gated = (cotangent[0].astype(jnp.float32) * gain[:, None, :]).astype(jnp.bfloat16)
    gathered = lax.all_gather(gated, "head", axis=0, tiled=False).reshape(-1, model)

    kv_send = [
        jnp.stack([columns_for(a, s, 0, width) for a in (key_rows, value_rows)]) for s in shifts
    ]
    kv_send, o_pieces = after(kv_send, o_pieces)
    kv = [rotated(a, "head", s) for s, a in zip(shifts, kv_send)]

    o = jnp.zeros((parts, frames, rows, width), jnp.bfloat16)
    for s, piece in enumerate([columns_for(saved_out, 0, 0, width)] + o_pieces):
        o = lax.dynamic_update_slice_in_dim(o, piece[None], lax.rem(me + parts - s, parts), axis=0)

    levels_xy = [("fsdp", 1 << i) for i in range(lax.axis_size("fsdp").bit_length() - 1)]
    levels_xy += [("frame", 1 << i) for i in range(lax.axis_size("frame").bit_length() - 2, 0, -1)]
    near = o.reshape(1, parts * frames * rows, width)
    flips = [(0, 0)]
    for axis, bit in levels_xy:
        near = jnp.concatenate([near, flipped(near, axis, bit)], axis=0)
        flips += [(a ^ bit, b) if axis == "frame" else (a, b ^ bit) for a, b in flips]
    far = flipped(near, "frame", 1)
    my_frame, my_video = lax.axis_index("frame"), lax.axis_index("fsdp")
    videos = lax.axis_size("fsdp")
    table = jnp.stack(
        [
            jnp.stack([(my_frame ^ (a ^ c)) * videos + (my_video ^ b) for a, b in flips])
            for c in range(2)
        ]
    ).astype(jnp.int32)

    gated_out = jnp.stack([gathered[:, b * block : (b + 1) * block] for b in range(blocks)])
    gated_in = lax.all_to_all(
        gated_out, ("frame", "fsdp"), split_axis=0, concat_axis=0, tiled=True
    )
    d_weight = weight_grad(table, near, far, gated_in, 1.0 / tokens_all)
    d = dot(gathered, out_weight, NT).astype(jnp.bfloat16).reshape(parts, frames, rows, width)

    first = (heads + 1) // 2
    groups = [(0, first), (first, heads - first)]
    q_send = [
        [columns_for(queries, s, head0 * HD, count * HD) for s in shifts]
        for head0, count in groups
    ]
    q_send, kv = after(q_send, kv)
    q_pieces = [[rotated(a, "head", s) for s, a in zip(shifts, sends)] for sends in q_send]

    ids = first_frame + jnp.arange(frames, dtype=jnp.int32)
    chosen = lax.dynamic_slice_in_dim(reach_flags, first_frame, frames, axis=0)
    inside = jnp.stack([ids > 0, ids < frames_all - 1], axis=1)
    limits = jnp.where(inside, jnp.where(chosen == 1, tokens, tokens // 2), 0).astype(jnp.int32)
    scal = jnp.concatenate([jnp.stack([me, me * heads]).astype(jnp.int32), limits.reshape(-1)])

    own = [columns_for(a, 0, 0, width) for a in (key_rows, value_rows)]

    def boundary(frame):
        return jnp.stack(
            [jnp.stack([own[t][frame]] + [p[t, frame] for p in kv]) for t in range(2)]
        )

    from_prev = shifted(boundary(frames - 1), "frame", 1)
    from_next = shifted(boundary(0), "frame", -1)
    local = (queries, key_rows, value_rows)
    results = []
    for (head0, count), q_group in zip(groups, q_pieces):
        if results:
            q_group, results[-1][0] = after(q_group, results[-1][0])
        dq, dk, dv, to_prev, to_next = attention(
            scal, head0, count, local, kv, q_group, o, d, from_prev, from_next
        )
        grad_next = shifted(to_prev, "frame", -1)
        grad_prev = shifted(to_next, "frame", 1)
        results.append([dq, dk, dv, grad_prev, grad_next])

    def combine(own_grad, t, grad_prev, grad_next):
        terms = [own_grad[f] for f in range(frames)]
        terms[0] = terms[0] + grad_prev[t].astype(jnp.float32)
        terms[frames - 1] = terms[frames - 1] + grad_next[t].astype(jnp.float32)
        return jnp.stack(terms).astype(jnp.bfloat16)

    d_queries = jnp.concatenate([r[0] for r in results], axis=2)[None]
    d_keys = jnp.concatenate([combine(r[1], 0, r[3], r[4]) for r in results], axis=2)[None]
    d_values = jnp.concatenate([combine(r[2], 1, r[3], r[4]) for r in results], axis=2)[None]
    return d_queries, d_keys, d_values, d_weight


def solution(mesh):
    rows = P("fsdp", "frame", "head", None)
    heads = P("fsdp", "frame", None, "head")
    in_specs = (rows, rows, rows, rows, rows, P("head", None), P(), P("frame"), P())
    out_specs = (heads, heads, heads, P("head", ("frame", "fsdp")))
    return jax.shard_map(
        per_device, mesh=mesh, in_specs=in_specs, out_specs=out_specs, check_vma=False
    )
```

```python
from functools import partial

import jax
import jax.numpy as jnp
from jax import lax
from jax.experimental import pallas as pl
from jax.experimental.pallas import tpu as pltpu
from jax.sharding import PartitionSpec as P

HD = 128
NEG = -1e30
NT = (((1,), (1,)), ((), ()))
NN = (((1,), (0,)), ((), ()))
TN = (((0,), (0,)), ((), ()))


def dot(lhs, rhs, dims):
    return lax.dot_general(lhs, rhs, dims, preferred_element_type=jnp.float32)


def attention_kernel(parts, scal, *refs):
    own_q, own_k, own_v = refs[:3]
    others, refs = parts - 1, refs[3:]
    kv_refs, q_refs, refs = refs[:others], refs[others : 2 * others], refs[2 * others :]
    o_ref, d_ref, prev_ref, next_ref, dq_ref, dk_ref, dv_ref, to_prev_ref, to_next_ref = refs[:9]
    q_all, k_all, v_all = refs[9:]
    _, frames, rows, _ = own_q.shape
    me = scal[0]
    inv_root = HD ** (-0.5)
    for s in range(parts):
        source = lax.rem(me + parts - s, parts)
        at = pl.ds(pl.multiple_of(source * rows, rows), rows)
        for f in range(frames):
            q_all[f, at] = own_q[0, f] if s == 0 else q_refs[s - 1][f]
            k_all[f + 1, at] = own_k[0, f] if s == 0 else kv_refs[s - 1][0, f]
            v_all[f + 1, at] = own_v[0, f] if s == 0 else kv_refs[s - 1][1, f]
        k_all[0, at] = prev_ref[0, s]
        v_all[0, at] = prev_ref[1, s]
        k_all[frames + 1, at] = next_ref[0, s]
        v_all[frames + 1, at] = next_ref[1, s]
    tokens = rows * parts
    row = lax.broadcasted_iota(jnp.int32, (tokens, tokens), 0)
    key_grads = [None] * (frames + 2)
    value_grads = [None] * (frames + 2)

    def put(grads, slot, term):
        grads[slot] = term if grads[slot] is None else grads[slot] + term

    for f in range(frames):
        q, d = q_all[f], d_ref[:, f].reshape(tokens, HD)
        prod = d.astype(jnp.float32) * o_ref[:, f].reshape(tokens, HD).astype(jnp.float32)
        delta = lax.dot_general(
            jnp.ones((8, HD), jnp.float32), prod, NT,
            precision=lax.Precision.HIGHEST, preferred_element_type=jnp.float32,
        )[0:1]
        scores = []
        for w in range(3):
            s = dot(k_all[f + w], q, NT) * inv_root
            if w != 1:
                s = jnp.where(row < scal[2 + 2 * f + w // 2], s, NEG)
            scores.append(s)
        top = jnp.max(jnp.maximum(jnp.maximum(scores[0], scores[1]), scores[2]), axis=0, keepdims=True)
        exps = [jnp.exp(s - top) for s in scores]
        total = jnp.sum(exps[0] + exps[1] + exps[2], axis=0, keepdims=True)
        inv_total = 1.0 / total
        dq = None
        for w in range(3):
            prob = exps[w] * inv_total
            put(value_grads, f + w, dot(prob.astype(jnp.bfloat16), d, NN))
            d_prob = dot(v_all[f + w], d, NT)
            d_score = (prob * (d_prob - delta)).astype(jnp.bfloat16)
            put(key_grads, f + w, dot(d_score, q, NN))
            term = dot(d_score, k_all[f + w], TN)
            dq = term if dq is None else dq + term
        dq_ref[f] = (dq * inv_root).astype(jnp.bfloat16)
    for f in range(frames):
        dk_ref[f] = key_grads[f + 1] * inv_root
        dv_ref[f] = value_grads[f + 1]
    to_prev_ref[0] = (key_grads[0] * inv_root).astype(jnp.bfloat16)
    to_prev_ref[1] = value_grads[0].astype(jnp.bfloat16)
    to_next_ref[0] = (key_grads[frames + 1] * inv_root).astype(jnp.bfloat16)
    to_next_ref[1] = value_grads[frames + 1].astype(jnp.bfloat16)


def attention(scal, head0, heads, local, kv, q_pieces, o, d, from_prev, from_next):
    parts = len(kv) + 1
    _, frames, rows, _ = local[0].shape
    tokens, width = parts * rows, heads * HD
    own = pl.BlockSpec((1, frames, rows, HD), lambda h, sc: (0, 0, 0, sc[1] + head0 + h))
    pack = pl.BlockSpec((2, frames, rows, HD), lambda h, sc: (0, 0, 0, head0 + h))
    q_spec = pl.BlockSpec((frames, rows, HD), lambda h, sc: (0, 0, h))
    dsp = pl.BlockSpec((parts, frames, rows, HD), lambda h, sc: (0, 0, 0, head0 + h))
    halo = pl.BlockSpec((2, parts, rows, HD), lambda h, sc: (0, 0, 0, head0 + h))
    out = pl.BlockSpec((frames, tokens, HD), lambda h, sc: (0, 0, h))
    edge = pl.BlockSpec((2, tokens, HD), lambda h, sc: (0, 0, h))
    full_shape, edge_shape = (frames, tokens, width), (2, tokens, width)
    pads = pltpu.VMEM((frames + 2, tokens, HD), jnp.bfloat16)
    flats = pltpu.VMEM((frames, tokens, HD), jnp.bfloat16)
    return pl.pallas_call(
        partial(attention_kernel, parts),
        grid_spec=pltpu.PrefetchScalarGridSpec(
            num_scalar_prefetch=1,
            grid=(heads,),
            in_specs=[own] * 3
            + [pack] * (parts - 1)
            + [q_spec] * (parts - 1)
            + [dsp, dsp, halo, halo],
            out_specs=[out] * 3 + [edge] * 2,
            scratch_shapes=[flats, pads, pads],
        ),
        out_shape=[
            jax.ShapeDtypeStruct(full_shape, jnp.bfloat16),
            jax.ShapeDtypeStruct(full_shape, jnp.float32),
            jax.ShapeDtypeStruct(full_shape, jnp.float32),
            jax.ShapeDtypeStruct(edge_shape, jnp.bfloat16),
            jax.ShapeDtypeStruct(edge_shape, jnp.bfloat16),
        ],
        compiler_params=pltpu.CompilerParams(vmem_limit_bytes=40 * 2**20),
        cost_estimate=pl.CostEstimate(
            flops=heads * frames * 3 * tokens * tokens * HD * 10,
            bytes_accessed=heads * HD * tokens * frames * 2 * 16,
            transcendentals=heads * frames * 3 * tokens * tokens,
        ),
        name="attention_backward",
    )(scal, *local, *kv, *q_pieces, o, d, from_prev, from_next)


def shifted(array, axis, step):
    count = lax.axis_size(axis)
    pairs = [(i, i + step) for i in range(count) if 0 <= i + step < count]
    return lax.ppermute(array, axis, pairs)


def rotated(array, axis, step):
    count = lax.axis_size(axis)
    return lax.ppermute(array, axis, [(i, (i + step) % count) for i in range(count)])


def after(array, event):
    return lax.optimization_barrier((array, event))


def flipped(array, axis, bit):
    return lax.ppermute(array, axis, [(i, i ^ bit) for i in range(lax.axis_size(axis))])


def weight_kernel(scale, table, near_ref, far_ref, g_near, g_far, out_ref):
    step = pl.program_id(0)

    @pl.when(step == 0)
    def _():
        out_ref[...] = jnp.zeros_like(out_ref)

    total = dot(near_ref[0], g_near[0], TN) + dot(far_ref[0], g_far[0], TN)
    out_ref[...] += total * scale


def weight_grad(table, near, far, gated, scale):
    count, rows, width = near.shape
    columns = gated.shape[2]
    side = pl.BlockSpec((1, rows, width), lambda j, tab: (j, 0, 0))
    return pl.pallas_call(
        partial(weight_kernel, scale),
        grid_spec=pltpu.PrefetchScalarGridSpec(
            num_scalar_prefetch=1,
            grid=(count,),
            in_specs=[
                side,
                side,
                pl.BlockSpec((1, rows, columns), lambda j, tab: (tab[0, j], 0, 0)),
                pl.BlockSpec((1, rows, columns), lambda j, tab: (tab[1, j], 0, 0)),
            ],
            out_specs=pl.BlockSpec((width, columns), lambda j, tab: (0, 0)),
        ),
        out_shape=jax.ShapeDtypeStruct((width, columns), jnp.float32),
        compiler_params=pltpu.CompilerParams(vmem_limit_bytes=40 * 2**20),
        cost_estimate=pl.CostEstimate(
            flops=4 * count * rows * width * columns,
            bytes_accessed=4 * count * rows * (width + columns) + 4 * width * columns,
            transcendentals=0,
        ),
        name="weight_gradient",
    )(table, near, far, gated, gated)


def project_kernel(g_ref, w_ref, out_ref, acc_ref):
    step = pl.program_id(0)
    term = dot(g_ref[0], w_ref[...], NT)

    @pl.when(step == 0)
    def _():
        acc_ref[...] = term

    @pl.when(step > 0)
    def _():
        acc_ref[...] += term

    @pl.when(step == pl.num_programs(0) - 1)
    def _():
        out_ref[...] = acc_ref[...].astype(out_ref.dtype)


def project(gated, weight):
    blocks, rows, columns = gated.shape
    width = weight.shape[0]
    if columns % 128:
        whole = gated.transpose(1, 0, 2).reshape(rows, blocks * columns)
        return dot(whole, weight, NT).astype(jnp.bfloat16)
    return pl.pallas_call(
        project_kernel,
        grid=(blocks,),
        in_specs=[
            pl.BlockSpec((1, rows, columns), lambda b: (b, 0, 0)),
            pl.BlockSpec((width, columns), lambda b: (0, b)),
        ],
        out_specs=pl.BlockSpec((rows, width), lambda b: (0, 0)),
        out_shape=jax.ShapeDtypeStruct((rows, width), jnp.bfloat16),
        scratch_shapes=[pltpu.VMEM((rows, width), jnp.float32)],
        compiler_params=pltpu.CompilerParams(vmem_limit_bytes=40 * 2**20),
        cost_estimate=pl.CostEstimate(
            flops=2 * rows * width * blocks * columns,
            bytes_accessed=2 * (rows + width) * blocks * columns + 2 * rows * width,
            transcendentals=0,
        ),
        name="project_gated",
    )(gated, weight)


def per_device(
    queries, key_rows, value_rows, saved_out, cotangent, out_weight, gate_table, levels, reach_flags
):
    _, frames, rows, model = queries.shape
    parts = lax.axis_size("head")
    me = lax.axis_index("head")
    width = model // parts
    heads = width // HD
    frames_all = frames * lax.axis_size("frame")
    tokens = rows * parts
    first_frame = lax.axis_index("frame") * frames
    tokens_all = lax.axis_size("fsdp") * frames_all * tokens
    blocks = lax.axis_size("frame") * lax.axis_size("fsdp")
    block = model // blocks
    def columns_for(array, step, start, size):
        target = lax.rem(me + step, parts)
        return lax.dynamic_slice_in_dim(array[0], target * width + start, size, axis=2)

    shifts = range(1, parts)
    shifts = range(1, parts)
    o_pieces = [rotated(columns_for(saved_out, s, 0, width), "head", s) for s in shifts]

    gain = jnp.concatenate(
        [lax.dynamic_slice_in_dim(gate_table, levels[f], 1, axis=0) for f in range(frames)], axis=0
    )
    gated = (cotangent[0].astype(jnp.float32) * gain[:, None, :]).astype(jnp.bfloat16)
    gated = gated.reshape(frames * rows, model)
    gated = jnp.stack([gated[:, b * block : (b + 1) * block] for b in range(blocks)])
    gathered = lax.all_gather(gated, "head", axis=1, tiled=True)

    kv_send = [
        jnp.stack([columns_for(a, s, 0, width) for a in (key_rows, value_rows)]) for s in shifts
    ]
    kv_send, gathered = after(kv_send, gathered)
    kv = [rotated(a, "head", s) for s, a in zip(shifts, kv_send)]

    o = jnp.zeros((parts, frames, rows, width), jnp.bfloat16)
    for s, piece in enumerate([columns_for(saved_out, 0, 0, width)] + o_pieces):
        o = lax.dynamic_update_slice_in_dim(o, piece[None], lax.rem(me + parts - s, parts), axis=0)

    levels_xy = [("fsdp", 1 << i) for i in range(lax.axis_size("fsdp").bit_length() - 1)]
    levels_xy += [("frame", 1 << i) for i in range(lax.axis_size("frame").bit_length() - 2, 0, -1)]
    near = o.reshape(1, parts * frames * rows, width)
    flips = [(0, 0)]
    for axis, bit in levels_xy:
        near = jnp.concatenate([near, flipped(near, axis, bit)], axis=0)
        flips += [(a ^ bit, b) if axis == "frame" else (a, b ^ bit) for a, b in flips]
    far = flipped(near, "frame", 1)
    my_frame, my_video = lax.axis_index("frame"), lax.axis_index("fsdp")
    videos = lax.axis_size("fsdp")
    table = jnp.stack(
        [
            jnp.stack([(my_frame ^ (a ^ c)) * videos + (my_video ^ b) for a, b in flips])
            for c in range(2)
        ]
    ).astype(jnp.int32)

    gated_in = lax.all_to_all(
        gathered, ("frame", "fsdp"), split_axis=0, concat_axis=0, tiled=True
    )
    d_weight = weight_grad(table, near, far, gated_in, 1.0 / tokens_all)
    d = project(gathered, out_weight)

    first = (heads + 1) // 2
    groups = [(0, first), (first, heads - first)]
    q_send = [
        [columns_for(queries, s, head0 * HD, count * HD) for s in shifts]
        for head0, count in groups
    ]
    q_send, d = after(q_send, d)
    kv, d = after(kv, d)
    d = d.reshape(parts, frames, rows, width)
    q_pieces = [[rotated(a, "head", s) for s, a in zip(shifts, sends)] for sends in q_send]

    ids = first_frame + jnp.arange(frames, dtype=jnp.int32)
    chosen = lax.dynamic_slice_in_dim(reach_flags, first_frame, frames, axis=0)
    inside = jnp.stack([ids > 0, ids < frames_all - 1], axis=1)
    limits = jnp.where(inside, jnp.where(chosen == 1, tokens, tokens // 2), 0).astype(jnp.int32)
    scal = jnp.concatenate([jnp.stack([me, me * heads]).astype(jnp.int32), limits.reshape(-1)])

    own = [columns_for(a, 0, 0, width) for a in (key_rows, value_rows)]

    def boundary(frame):
        return jnp.stack(
            [jnp.stack([own[t][frame]] + [p[t, frame] for p in kv]) for t in range(2)]
        )

    from_prev = shifted(boundary(frames - 1), "frame", 1)
    from_next = shifted(boundary(0), "frame", -1)
    local = (queries, key_rows, value_rows)
    scal, d_weight = after(scal, d_weight)
    results = []
    for (head0, count), q_group in zip(groups, q_pieces):
        if results:
            q_group, results[-1][0] = after(q_group, results[-1][0])
        dq, dk, dv, to_prev, to_next = attention(
            scal, head0, count, local, kv, q_group, o, d, from_prev, from_next
        )
        grad_next = shifted(to_prev, "frame", -1)
        grad_prev = shifted(to_next, "frame", 1)
        results.append([dq, dk, dv, grad_prev, grad_next])

    def combine(own_grad, t, grad_prev, grad_next):
        terms = [own_grad[f] for f in range(frames)]
        terms[0] = terms[0] + grad_prev[t].astype(jnp.float32)
        terms[frames - 1] = terms[frames - 1] + grad_next[t].astype(jnp.float32)
        return jnp.stack(terms).astype(jnp.bfloat16)

    d_queries = jnp.concatenate([r[0] for r in results], axis=2)[None]
    d_keys = jnp.concatenate([combine(r[1], 0, r[3], r[4]) for r in results], axis=2)[None]
    d_values = jnp.concatenate([combine(r[2], 1, r[3], r[4]) for r in results], axis=2)[None]
    return d_queries, d_keys, d_values, d_weight


def solution(mesh):
    rows = P("fsdp", "frame", "head", None)
    heads = P("fsdp", "frame", None, "head")
    in_specs = (rows, rows, rows, rows, rows, P("head", None), P(), P("frame"), P())
    out_specs = (heads, heads, heads, P("head", ("frame", "fsdp")))
    return jax.shard_map(
        per_device, mesh=mesh, in_specs=in_specs, out_specs=out_specs, check_vma=False
    )
```

```python
from functools import partial

import jax
import jax.numpy as jnp
from jax import lax
from jax.experimental import pallas as pl
from jax.experimental.pallas import tpu as pltpu
from jax.sharding import PartitionSpec as P

HD = 128
NEG = -1e30
NT = (((1,), (1,)), ((), ()))
NN = (((1,), (0,)), ((), ()))
TN = (((0,), (0,)), ((), ()))


def dot(lhs, rhs, dims):
    return lax.dot_general(lhs, rhs, dims, preferred_element_type=jnp.float32)


def attention_kernel(parts, scal, *refs):
    own_q, own_k, own_v = refs[:3]
    others, refs = parts - 1, refs[3:]
    kv_refs, q_refs, refs = refs[:others], refs[others : 2 * others], refs[2 * others :]
    o_ref, d_ref, prev_ref, next_ref, dq_ref, dk_ref, dv_ref, to_prev_ref, to_next_ref = refs[:9]
    q_all, k_all, v_all = refs[9:]
    _, frames, rows, _ = own_q.shape
    me = scal[0]
    inv_root = HD ** (-0.5)
    for s in range(parts):
        source = lax.rem(me + parts - s, parts)
        at = pl.ds(pl.multiple_of(source * rows, rows), rows)
        for f in range(frames):
            q_all[f, at] = own_q[0, f] if s == 0 else q_refs[s - 1][f]
            k_all[f + 1, at] = own_k[0, f] if s == 0 else kv_refs[s - 1][0, f]
            v_all[f + 1, at] = own_v[0, f] if s == 0 else kv_refs[s - 1][1, f]
        k_all[0, at] = prev_ref[0, s]
        v_all[0, at] = prev_ref[1, s]
        k_all[frames + 1, at] = next_ref[0, s]
        v_all[frames + 1, at] = next_ref[1, s]
    tokens = rows * parts
    row = lax.broadcasted_iota(jnp.int32, (tokens, tokens), 0)
    key_grads = [None] * (frames + 2)
    value_grads = [None] * (frames + 2)

    def put(grads, slot, term):
        grads[slot] = term if grads[slot] is None else grads[slot] + term

    for f in range(frames):
        q, d = q_all[f], d_ref[:, f].reshape(tokens, HD)
        prod = d.astype(jnp.float32) * o_ref[:, f].reshape(tokens, HD).astype(jnp.float32)
        delta = lax.dot_general(
            jnp.ones((8, HD), jnp.float32), prod, NT,
            precision=lax.Precision.HIGHEST, preferred_element_type=jnp.float32,
        )[0:1]
        scores = []
        for w in range(3):
            s = dot(k_all[f + w], q, NT) * inv_root
            if w != 1:
                s = jnp.where(row < scal[2 + 2 * f + w // 2], s, NEG)
            scores.append(s)
        top = jnp.max(jnp.maximum(jnp.maximum(scores[0], scores[1]), scores[2]), axis=0, keepdims=True)
        exps = [jnp.exp(s - top) for s in scores]
        total = jnp.sum(exps[0] + exps[1] + exps[2], axis=0, keepdims=True)
        inv_total = 1.0 / total
        dq = None
        for w in range(3):
            prob = exps[w] * inv_total
            put(value_grads, f + w, dot(prob.astype(jnp.bfloat16), d, NN))
            d_prob = dot(v_all[f + w], d, NT)
            d_score = (prob * (d_prob - delta)).astype(jnp.bfloat16)
            put(key_grads, f + w, dot(d_score, q, NN))
            term = dot(d_score, k_all[f + w], TN)
            dq = term if dq is None else dq + term
        dq_ref[f] = (dq * inv_root).astype(jnp.bfloat16)
    for f in range(frames):
        dk_ref[f] = key_grads[f + 1] * inv_root
        dv_ref[f] = value_grads[f + 1]
    to_prev_ref[0] = (key_grads[0] * inv_root).astype(jnp.bfloat16)
    to_prev_ref[1] = value_grads[0].astype(jnp.bfloat16)
    to_next_ref[0] = (key_grads[frames + 1] * inv_root).astype(jnp.bfloat16)
    to_next_ref[1] = value_grads[frames + 1].astype(jnp.bfloat16)


def attention(scal, head0, heads, local, kv, q_pieces, o, d, from_prev, from_next):
    parts = len(kv) + 1
    _, frames, rows, _ = local[0].shape
    tokens, width = parts * rows, heads * HD
    own = pl.BlockSpec((1, frames, rows, HD), lambda h, sc: (0, 0, 0, sc[1] + head0 + h))
    pack = pl.BlockSpec((2, frames, rows, HD), lambda h, sc: (0, 0, 0, head0 + h))
    q_spec = pl.BlockSpec((frames, rows, HD), lambda h, sc: (0, 0, h))
    dsp = pl.BlockSpec((parts, frames, rows, HD), lambda h, sc: (0, 0, 0, head0 + h))
    halo = pl.BlockSpec((2, parts, rows, HD), lambda h, sc: (0, 0, 0, head0 + h))
    out = pl.BlockSpec((frames, tokens, HD), lambda h, sc: (0, 0, h))
    edge = pl.BlockSpec((2, tokens, HD), lambda h, sc: (0, 0, h))
    full_shape, edge_shape = (frames, tokens, width), (2, tokens, width)
    pads = pltpu.VMEM((frames + 2, tokens, HD), jnp.bfloat16)
    flats = pltpu.VMEM((frames, tokens, HD), jnp.bfloat16)
    return pl.pallas_call(
        partial(attention_kernel, parts),
        grid_spec=pltpu.PrefetchScalarGridSpec(
            num_scalar_prefetch=1,
            grid=(heads,),
            in_specs=[own] * 3
            + [pack] * (parts - 1)
            + [q_spec] * (parts - 1)
            + [dsp, dsp, halo, halo],
            out_specs=[out] * 3 + [edge] * 2,
            scratch_shapes=[flats, pads, pads],
        ),
        out_shape=[
            jax.ShapeDtypeStruct(full_shape, jnp.bfloat16),
            jax.ShapeDtypeStruct(full_shape, jnp.float32),
            jax.ShapeDtypeStruct(full_shape, jnp.float32),
            jax.ShapeDtypeStruct(edge_shape, jnp.bfloat16),
            jax.ShapeDtypeStruct(edge_shape, jnp.bfloat16),
        ],
        compiler_params=pltpu.CompilerParams(vmem_limit_bytes=40 * 2**20),
        cost_estimate=pl.CostEstimate(
            flops=heads * frames * 3 * tokens * tokens * HD * 10,
            bytes_accessed=heads * HD * tokens * frames * 2 * 16,
            transcendentals=heads * frames * 3 * tokens * tokens,
        ),
        name="attention_backward",
    )(scal, *local, *kv, *q_pieces, o, d, from_prev, from_next)


def shifted(array, axis, step):
    count = lax.axis_size(axis)
    pairs = [(i, i + step) for i in range(count) if 0 <= i + step < count]
    return lax.ppermute(array, axis, pairs)


def rotated(array, axis, step):
    count = lax.axis_size(axis)
    return lax.ppermute(array, axis, [(i, (i + step) % count) for i in range(count)])


def after(array, event):
    return lax.optimization_barrier((array, event))


def flipped(array, axis, bit):
    return lax.ppermute(array, axis, [(i, i ^ bit) for i in range(lax.axis_size(axis))])


def weight_kernel(scale, table, near_ref, far_ref, g_near, g_far, out_ref):
    step = pl.program_id(0)

    @pl.when(step == 0)
    def _():
        out_ref[...] = jnp.zeros_like(out_ref)

    total = dot(near_ref[0], g_near[0], TN) + dot(far_ref[0], g_far[0], TN)
    out_ref[...] += total * scale


def weight_grad(table, near, far, gated, scale):
    count, rows, width = near.shape
    columns = gated.shape[2]
    side = pl.BlockSpec((1, rows, width), lambda j, tab: (j, 0, 0))
    return pl.pallas_call(
        partial(weight_kernel, scale),
        grid_spec=pltpu.PrefetchScalarGridSpec(
            num_scalar_prefetch=1,
            grid=(count,),
            in_specs=[
                side,
                side,
                pl.BlockSpec((1, rows, columns), lambda j, tab: (tab[0, j], 0, 0)),
                pl.BlockSpec((1, rows, columns), lambda j, tab: (tab[1, j], 0, 0)),
            ],
            out_specs=pl.BlockSpec((width, columns), lambda j, tab: (0, 0)),
        ),
        out_shape=jax.ShapeDtypeStruct((width, columns), jnp.float32),
        compiler_params=pltpu.CompilerParams(vmem_limit_bytes=40 * 2**20),
        cost_estimate=pl.CostEstimate(
            flops=4 * count * rows * width * columns,
            bytes_accessed=4 * count * rows * (width + columns) + 4 * width * columns,
            transcendentals=0,
        ),
        name="weight_gradient",
    )(table, near, far, gated, gated)


def project_kernel(g_ref, w_ref, out_ref, acc_ref):
    step = pl.program_id(0)
    term = dot(g_ref[0], w_ref[...], NT)

    @pl.when(step == 0)
    def _():
        acc_ref[...] = term

    @pl.when(step > 0)
    def _():
        acc_ref[...] += term

    @pl.when(step == pl.num_programs(0) - 1)
    def _():
        out_ref[...] = acc_ref[...].astype(out_ref.dtype)


def project(gated, weight):
    blocks, rows, columns = gated.shape
    width = weight.shape[0]
    if columns % 128:
        whole = gated.transpose(1, 0, 2).reshape(rows, blocks * columns)
        return dot(whole, weight, NT).astype(jnp.bfloat16)
    return pl.pallas_call(
        project_kernel,
        grid=(blocks,),
        in_specs=[
            pl.BlockSpec((1, rows, columns), lambda b: (b, 0, 0)),
            pl.BlockSpec((width, columns), lambda b: (0, b)),
        ],
        out_specs=pl.BlockSpec((rows, width), lambda b: (0, 0)),
        out_shape=jax.ShapeDtypeStruct((rows, width), jnp.bfloat16),
        scratch_shapes=[pltpu.VMEM((rows, width), jnp.float32)],
        compiler_params=pltpu.CompilerParams(vmem_limit_bytes=40 * 2**20),
        cost_estimate=pl.CostEstimate(
            flops=2 * rows * width * blocks * columns,
            bytes_accessed=2 * (rows + width) * blocks * columns + 2 * rows * width,
            transcendentals=0,
        ),
        name="project_gated",
    )(gated, weight)


def per_device(
    queries, key_rows, value_rows, saved_out, cotangent, out_weight, gate_table, levels, reach_flags
):
    _, frames, rows, model = queries.shape
    parts = lax.axis_size("head")
    me = lax.axis_index("head")
    width = model // parts
    heads = width // HD
    frames_all = frames * lax.axis_size("frame")
    tokens = rows * parts
    first_frame = lax.axis_index("frame") * frames
    tokens_all = lax.axis_size("fsdp") * frames_all * tokens
    blocks = lax.axis_size("frame") * lax.axis_size("fsdp")
    block = model // blocks
    def columns_for(array, step, start, size):
        target = lax.rem(me + step, parts)
        return lax.dynamic_slice_in_dim(array[0], target * width + start, size, axis=2)

    shifts = range(1, parts)
    shifts = range(1, parts)
    o_pieces = [rotated(columns_for(saved_out, s, 0, width), "head", s) for s in shifts]

    gain = jnp.concatenate(
        [lax.dynamic_slice_in_dim(gate_table, levels[f], 1, axis=0) for f in range(frames)], axis=0
    )
    gated = (cotangent[0].astype(jnp.float32) * gain[:, None, :]).astype(jnp.bfloat16)
    gated = gated.reshape(frames * rows, model)
    gated = jnp.stack([gated[:, b * block : (b + 1) * block] for b in range(blocks)])

    kv_send = [
        jnp.stack([columns_for(a, s, 0, width) for a in (key_rows, value_rows)]) for s in shifts
    ]
    kv = [rotated(a, "head", s) for s, a in zip(shifts, kv_send)]
    gated, o_pieces, kv = lax.optimization_barrier((gated, o_pieces, kv))
    gathered = lax.all_gather(gated, "head", axis=1, tiled=True)

    own = [columns_for(a, 0, 0, width) for a in (key_rows, value_rows)]

    def boundary(frame):
        return jnp.stack(
            [jnp.stack([own[t][frame]] + [p[t, frame] for p in kv]) for t in range(2)]
        )

    from_prev = shifted(boundary(frames - 1), "frame", 1)
    from_next = shifted(boundary(0), "frame", -1)
    halos = (from_prev, from_next)

    o = jnp.zeros((parts, frames, rows, width), jnp.bfloat16)
    for s, piece in enumerate([columns_for(saved_out, 0, 0, width)] + o_pieces):
        o = lax.dynamic_update_slice_in_dim(o, piece[None], lax.rem(me + parts - s, parts), axis=0)

    levels_xy = [("fsdp", 1 << i) for i in range(lax.axis_size("fsdp").bit_length() - 1)]
    levels_xy += [("frame", 1 << i) for i in range(lax.axis_size("frame").bit_length() - 2, 0, -1)]
    near = o.reshape(1, parts * frames * rows, width)
    flips = [(0, 0)]
    for axis, bit in levels_xy:
        if (axis, bit) == levels_xy[-1]:
            near, halos = after(near, halos)
        near = jnp.concatenate([near, flipped(near, axis, bit)], axis=0)
        flips += [(a ^ bit, b) if axis == "frame" else (a, b ^ bit) for a, b in flips]
    far = flipped(near, "frame", 1)
    my_frame, my_video = lax.axis_index("frame"), lax.axis_index("fsdp")
    videos = lax.axis_size("fsdp")
    table = jnp.stack(
        [
            jnp.stack([(my_frame ^ (a ^ c)) * videos + (my_video ^ b) for a, b in flips])
            for c in range(2)
        ]
    ).astype(jnp.int32)

    gated_in = lax.all_to_all(
        gathered, ("frame", "fsdp"), split_axis=0, concat_axis=0, tiled=True
    )
    d_weight = weight_grad(table, near, far, gated_in, 1.0 / tokens_all)
    d = project(gathered, out_weight)

    first = (heads + 1) // 2
    groups = [(0, first), (first, heads - first)]
    q_send = [
        [columns_for(queries, s, head0 * HD, count * HD) for s in shifts]
        for head0, count in groups
    ]
    q_send, gathered = after(q_send, gathered)
    d = d.reshape(parts, frames, rows, width)
    q_pieces = [[rotated(a, "head", s) for s, a in zip(shifts, sends)] for sends in q_send]

    ids = first_frame + jnp.arange(frames, dtype=jnp.int32)
    chosen = lax.dynamic_slice_in_dim(reach_flags, first_frame, frames, axis=0)
    inside = jnp.stack([ids > 0, ids < frames_all - 1], axis=1)
    limits = jnp.where(inside, jnp.where(chosen == 1, tokens, tokens // 2), 0).astype(jnp.int32)
    scal = jnp.concatenate([jnp.stack([me, me * heads]).astype(jnp.int32), limits.reshape(-1)])

    local = (queries, key_rows, value_rows)
    results = []
    for (head0, count), q_group in zip(groups, q_pieces):
        if results:
            q_group, results[-1][0] = after(q_group, results[-1][0])
        dq, dk, dv, to_prev, to_next = attention(
            scal, head0, count, local, kv, q_group, o, d, *halos
        )
        grad_next = shifted(to_prev, "frame", -1)
        grad_prev = shifted(to_next, "frame", 1)
        results.append([dq, dk, dv, grad_prev, grad_next])

    edges, d_weight = after([r[3:] for r in results], d_weight)
    results = [r[:3] + e for r, e in zip(results, edges)]

    def combine(own_grad, t, grad_prev, grad_next):
        terms = [own_grad[f] for f in range(frames)]
        terms[0] = terms[0] + grad_prev[t].astype(jnp.float32)
        terms[frames - 1] = terms[frames - 1] + grad_next[t].astype(jnp.float32)
        return jnp.stack(terms).astype(jnp.bfloat16)

    d_queries = jnp.concatenate([r[0] for r in results], axis=2)[None]
    d_keys = jnp.concatenate([combine(r[1], 0, r[3], r[4]) for r in results], axis=2)[None]
    d_values = jnp.concatenate([combine(r[2], 1, r[3], r[4]) for r in results], axis=2)[None]
    return d_queries, d_keys, d_values, d_weight


def solution(mesh):
    rows = P("fsdp", "frame", "head", None)
    heads = P("fsdp", "frame", None, "head")
    in_specs = (rows, rows, rows, rows, rows, P("head", None), P(), P("frame"), P())
    out_specs = (heads, heads, heads, P("head", ("frame", "fsdp")))
    return jax.shard_map(
        per_device, mesh=mesh, in_specs=in_specs, out_specs=out_specs, check_vma=False
    )
```

```python
from functools import partial

import jax
import jax.numpy as jnp
from jax import lax
from jax.experimental import pallas as pl
from jax.experimental.pallas import tpu as pltpu
from jax.sharding import PartitionSpec as P

HD = 128
NEG = -1e30
NT = (((1,), (1,)), ((), ()))
NN = (((1,), (0,)), ((), ()))
TN = (((0,), (0,)), ((), ()))


def dot(lhs, rhs, dims):
    return lax.dot_general(lhs, rhs, dims, preferred_element_type=jnp.float32)


def attention_kernel(parts, f, adds, scal, *refs):
    own_q, own_k, own_v = refs[:3]
    others, refs = parts - 1, refs[3:]
    kv_refs, q_refs, refs = refs[:others], refs[others : 2 * others], refs[2 * others :]
    o_ref, d_ref, prev_ref, next_ref = refs[:4]
    refs = refs[4:]
    add_refs = []
    for count in adds:
        add_refs.append(refs[:count])
        refs = refs[count:]
    dq_ref, slot_refs, (q_all, k_all, v_all) = refs[0], refs[1:4], refs[4:]
    _, frames, rows, _ = own_k.shape
    tokens = rows * parts
    me = scal[0]
    inv_root = HD ** (-0.5)
    for s in range(parts):
        source = lax.rem(me + parts - s, parts)
        at = pl.ds(pl.multiple_of(source * rows, rows), rows)
        q_all[at] = own_q[0, 0] if s == 0 else q_refs[s - 1][...]
        for w in range(3):
            frame = f + w - 1
            if frame < 0 or frame == frames:
                side = prev_ref if frame < 0 else next_ref
                k_all[w, at] = side[0, s]
                v_all[w, at] = side[1, s]
            else:
                k_all[w, at] = own_k[0, frame] if s == 0 else kv_refs[s - 1][0, frame]
                v_all[w, at] = own_v[0, frame] if s == 0 else kv_refs[s - 1][1, frame]
    row = lax.broadcasted_iota(jnp.int32, (tokens, tokens), 0)
    q, d = q_all[...], d_ref[...]
    prod = d.astype(jnp.float32) * o_ref[0].reshape(tokens, HD).astype(jnp.float32)
    delta = lax.dot_general(
        jnp.ones((8, HD), jnp.float32), prod, NT,
        precision=lax.Precision.HIGHEST, preferred_element_type=jnp.float32,
    )[0:1]
    scores = []
    for w in range(3):
        s = dot(k_all[w], q, NT) * inv_root
        if w != 1:
            s = jnp.where(row < scal[2 + 2 * f + w // 2], s, NEG)
        scores.append(s)
    top = jnp.max(jnp.maximum(jnp.maximum(scores[0], scores[1]), scores[2]), axis=0, keepdims=True)
    exps = [jnp.exp(s - top) for s in scores]
    total = jnp.sum(exps[0] + exps[1] + exps[2], axis=0, keepdims=True)
    inv_total = 1.0 / total
    dq = None
    for w in range(3):
        prob = exps[w] * inv_total
        d_value = dot(prob.astype(jnp.bfloat16), d, NN)
        d_prob = dot(v_all[w], d, NT)
        d_score = (prob * (d_prob - delta)).astype(jnp.bfloat16)
        d_key = dot(d_score, q, NN) * inv_root
        term = dot(d_score, k_all[w], TN)
        dq = term if dq is None else dq + term
        for ref in add_refs[w]:
            d_key += ref[0].astype(jnp.float32)
            d_value += ref[1].astype(jnp.float32)
        slot_refs[w][0] = d_key.astype(slot_refs[w].dtype)
        slot_refs[w][1] = d_value.astype(slot_refs[w].dtype)
    dq_ref[...] = (dq * inv_root).astype(jnp.bfloat16)


def attention(scal, f, local, kv, q_pieces, o, d, halos, adds, dtypes):
    parts = len(kv) + 1
    _, frames, rows, _ = local[0].shape
    tokens, width = d.shape
    heads = width // HD
    own_q = pl.BlockSpec((1, 1, rows, HD), lambda h, sc: (0, f, 0, sc[1] + h))
    own = pl.BlockSpec((1, frames, rows, HD), lambda h, sc: (0, 0, 0, sc[1] + h))
    pack = pl.BlockSpec((2, frames, rows, HD), lambda h, sc: (0, 0, 0, h))
    q_spec = pl.BlockSpec((rows, HD), lambda h, sc: (0, h))
    o_spec = pl.BlockSpec((1, parts, rows, HD), lambda h, sc: (f, 0, 0, h))
    flat = pl.BlockSpec((tokens, HD), lambda h, sc: (0, h))
    halo = pl.BlockSpec((2, parts, rows, HD), lambda h, sc: (0, 0, 0, h))
    pair = pl.BlockSpec((2, tokens, HD), lambda h, sc: (0, 0, h))
    flat_adds = [a for group in adds for a in group]
    pads = pltpu.VMEM((3, tokens, HD), jnp.bfloat16)
    return pl.pallas_call(
        partial(attention_kernel, parts, f, [len(group) for group in adds]),
        grid_spec=pltpu.PrefetchScalarGridSpec(
            num_scalar_prefetch=1,
            grid=(heads,),
            in_specs=[own_q, own, own]
            + [pack] * (parts - 1)
            + [q_spec] * (parts - 1)
            + [o_spec, flat, halo, halo]
            + [pair] * len(flat_adds),
            out_specs=[flat] + [pair] * 3,
            scratch_shapes=[pltpu.VMEM((tokens, HD), jnp.bfloat16), pads, pads],
        ),
        out_shape=[jax.ShapeDtypeStruct((tokens, width), jnp.bfloat16)]
        + [jax.ShapeDtypeStruct((2, tokens, width), t) for t in dtypes],
        compiler_params=pltpu.CompilerParams(vmem_limit_bytes=40 * 2**20),
        cost_estimate=pl.CostEstimate(
            flops=heads * 3 * tokens * tokens * HD * 10,
            bytes_accessed=heads * HD * tokens * 40,
            transcendentals=heads * 3 * tokens * tokens,
        ),
        name="attention_backward",
    )(scal, *local, *kv, *q_pieces, o, d, *halos, *flat_adds)


def shifted(array, axis, step):
    count = lax.axis_size(axis)
    pairs = [(i, i + step) for i in range(count) if 0 <= i + step < count]
    return lax.ppermute(array, axis, pairs)


def rotated(array, axis, step):
    count = lax.axis_size(axis)
    return lax.ppermute(array, axis, [(i, (i + step) % count) for i in range(count)])


def after(array, event):
    return lax.optimization_barrier((array, event))


def flipped(array, axis, bit):
    return lax.ppermute(array, axis, [(i, i ^ bit) for i in range(lax.axis_size(axis))])


def weight_kernel(scale, table, near_ref, far_ref, g_near, g_far, *refs):
    out_ref = refs[-1]

    @pl.when(pl.program_id(0) == 0)
    def _():
        out_ref[...] = refs[0][...] if len(refs) > 1 else jnp.zeros_like(out_ref)

    total = dot(near_ref[0], g_near[0], TN) + dot(far_ref[0], g_far[0], TN)
    out_ref[...] += total * scale


def weight_grad(table, f, near, far, gated, scale, before):
    count, _, width = near.shape
    _, rows, columns = gated.shape
    side = pl.BlockSpec((1, rows, width), lambda j, tab: (j, f, 0))
    whole = pl.BlockSpec((width, columns), lambda j, tab: (0, 0))
    return pl.pallas_call(
        partial(weight_kernel, scale),
        grid_spec=pltpu.PrefetchScalarGridSpec(
            num_scalar_prefetch=1,
            grid=(count,),
            in_specs=[
                side,
                side,
                pl.BlockSpec((1, rows, columns), lambda j, tab: (tab[0, j], 0, 0)),
                pl.BlockSpec((1, rows, columns), lambda j, tab: (tab[1, j], 0, 0)),
            ]
            + [whole] * len(before),
            out_specs=whole,
        ),
        out_shape=jax.ShapeDtypeStruct((width, columns), jnp.float32),
        compiler_params=pltpu.CompilerParams(vmem_limit_bytes=40 * 2**20),
        cost_estimate=pl.CostEstimate(
            flops=4 * count * rows * width * columns,
            bytes_accessed=4 * count * rows * (width + columns) + 4 * width * columns,
            transcendentals=0,
        ),
        name="weight_gradient",
    )(table, near, far, gated, gated, *before)


def project_kernel(g_ref, w_ref, out_ref, acc_ref):
    step = pl.program_id(0)
    term = dot(g_ref[0], w_ref[...], NT)

    @pl.when(step == 0)
    def _():
        acc_ref[...] = term

    @pl.when(step > 0)
    def _():
        acc_ref[...] += term

    @pl.when(step == pl.num_programs(0) - 1)
    def _():
        out_ref[...] = acc_ref[...].astype(out_ref.dtype)


def project(gated, weight):
    blocks, rows, columns = gated.shape
    width = weight.shape[0]
    if columns % 128:
        whole = gated.transpose(1, 0, 2).reshape(rows, blocks * columns)
        return dot(whole, weight, NT).astype(jnp.bfloat16)
    return pl.pallas_call(
        project_kernel,
        grid=(blocks,),
        in_specs=[
            pl.BlockSpec((1, rows, columns), lambda b: (b, 0, 0)),
            pl.BlockSpec((width, columns), lambda b: (0, b)),
        ],
        out_specs=pl.BlockSpec((rows, width), lambda b: (0, 0)),
        out_shape=jax.ShapeDtypeStruct((rows, width), jnp.bfloat16),
        scratch_shapes=[pltpu.VMEM((rows, width), jnp.float32)],
        compiler_params=pltpu.CompilerParams(vmem_limit_bytes=40 * 2**20),
        cost_estimate=pl.CostEstimate(
            flops=2 * rows * width * blocks * columns,
            bytes_accessed=2 * (rows + width) * blocks * columns + 2 * rows * width,
            transcendentals=0,
        ),
        name="project_gated",
    )(gated, weight)


def per_device(
    queries, key_rows, value_rows, saved_out, cotangent, out_weight, gate_table, levels, reach_flags
):
    _, frames, rows, model = queries.shape
    parts = lax.axis_size("head")
    me = lax.axis_index("head")
    width = model // parts
    heads = width // HD
    frames_all = frames * lax.axis_size("frame")
    tokens = rows * parts
    first_frame = lax.axis_index("frame") * frames
    tokens_all = lax.axis_size("fsdp") * frames_all * tokens
    blocks = lax.axis_size("frame") * lax.axis_size("fsdp")
    block = model // blocks
    def columns_for(array, step, start, size):
        target = lax.rem(me + step, parts)
        return lax.dynamic_slice_in_dim(array[0], target * width + start, size, axis=2)

    shifts = range(1, parts)
    o_pieces = [rotated(columns_for(saved_out, s, 0, width), "head", s) for s in shifts]

    gain = jnp.concatenate(
        [lax.dynamic_slice_in_dim(gate_table, levels[f], 1, axis=0) for f in range(frames)], axis=0
    )
    gated = (cotangent[0].astype(jnp.float32) * gain[:, None, :]).astype(jnp.bfloat16)
    gated = [
        jnp.stack([gated[f, :, b * block : (b + 1) * block] for b in range(blocks)])
        for f in range(frames)
    ]

    kv_send = [
        jnp.stack([columns_for(a, s, 0, width) for a in (key_rows, value_rows)]) for s in shifts
    ]
    q_send = [[columns_for(queries, s, 0, width)[f] for s in shifts] for f in range(frames)]
    kv_send, q_send[0], o_pieces = lax.optimization_barrier((kv_send, q_send[0], o_pieces))
    kv = [rotated(a, "head", s) for s, a in zip(shifts, kv_send)]
    q_pieces = [[rotated(a, "head", s) for s, a in zip(shifts, q_send[0])]]

    own = [columns_for(a, 0, 0, width) for a in (key_rows, value_rows)]

    def boundary(frame):
        return jnp.stack(
            [jnp.stack([own[t][frame]] + [p[t, frame] for p in kv]) for t in range(2)]
        )

    gated[0], q_pieces[0], kv = lax.optimization_barrier((gated[0], q_pieces[0], kv))
    halos = (
        shifted(boundary(frames - 1), "frame", 1),
        shifted(boundary(0), "frame", -1),
    )

    gathered = [lax.all_gather(gated[0], "head", axis=1, tiled=True)]
    for f in range(1, frames):
        gated[f], gathered[-1], halos = lax.optimization_barrier((gated[f], gathered[-1], halos))
        gathered.append(lax.all_gather(gated[f], "head", axis=1, tiled=True))
        q_send[f], gathered[f] = after(q_send[f], gathered[f])
        q_pieces.append([rotated(a, "head", s) for s, a in zip(shifts, q_send[f])])

    o = jnp.zeros((frames, parts, rows, width), jnp.bfloat16)
    for s, piece in enumerate([columns_for(saved_out, 0, 0, width)] + o_pieces):
        source = lax.rem(me + parts - s, parts)
        o = lax.dynamic_update_slice_in_dim(o, piece[:, None], source, axis=1)

    levels_xy = [("fsdp", 1 << i) for i in range(lax.axis_size("fsdp").bit_length() - 1)]
    levels_xy += [("frame", 1 << i) for i in range(lax.axis_size("frame").bit_length() - 2, 0, -1)]
    near = o.reshape(1, frames * parts * rows, width)
    flips = [(0, 0)]
    for axis, bit in levels_xy:
        near = jnp.concatenate([near, flipped(near, axis, bit)], axis=0)
        flips += [(a ^ bit, b) if axis == "frame" else (a, b ^ bit) for a, b in flips]
    far = flipped(near, "frame", 1)
    my_frame, my_video = lax.axis_index("frame"), lax.axis_index("fsdp")
    videos = lax.axis_size("fsdp")
    table = jnp.stack(
        [
            jnp.stack([(my_frame ^ (a ^ c)) * videos + (my_video ^ b) for a, b in flips])
            for c in range(2)
        ]
    ).astype(jnp.int32)

    ids = first_frame + jnp.arange(frames, dtype=jnp.int32)
    chosen = lax.dynamic_slice_in_dim(reach_flags, first_frame, frames, axis=0)
    inside = jnp.stack([ids > 0, ids < frames_all - 1], axis=1)
    limits = jnp.where(inside, jnp.where(chosen == 1, tokens, tokens // 2), 0).astype(jnp.int32)
    scal = jnp.concatenate([jnp.stack([me, me * heads]).astype(jnp.int32), limits.reshape(-1)])

    local = (queries, key_rows, value_rows)
    d_queries, done, before = [], [None] * frames, []
    own_part, next_part, from_next = None, None, None
    last = frames - 1
    for f in range(frames):
        columns = lax.all_to_all(
            gathered[f], ("frame", "fsdp"), split_axis=0, concat_axis=0, tiled=True
        )
        d = project(gathered[f], out_weight)
        d, before = after(d, before)
        adds = [[], [], []]
        if f > 0:
            adds = [[own_part], [next_part], []]
        if f > 0 and f == last:
            adds[1].append(from_next)
        exact, low = jnp.float32, jnp.bfloat16
        dtypes = [
            exact if f == 1 else low,
            low if f == last and f > 0 else exact,
            low if f == last else exact,
        ]
        dq, to_prev, own_part, next_part = attention(
            scal, f, local, kv, q_pieces[f], o, d, halos, adds, dtypes
        )
        d_queries.append(dq)
        if f == 0:
            from_next = shifted(to_prev, "frame", -1)
        else:
            done[f - 1] = to_prev
        before = [weight_grad(table, f, near, far, columns, 1.0 / tokens_all, before)]
    done[last] = own_part
    from_prev = shifted(next_part, "frame", 1)
    d_weight, from_prev = after(before[0], from_prev)
    done[0] = done[0].astype(jnp.float32) + from_prev.astype(jnp.float32)
    if last == 0:
        done[0] = done[0] + from_next.astype(jnp.float32)
    done = [pair.astype(jnp.bfloat16) for pair in done]
    d_keys, d_values = (jnp.stack([pair[t] for pair in done])[None] for t in range(2))
    return jnp.stack(d_queries)[None], d_keys, d_values, d_weight


def solution(mesh):
    rows = P("fsdp", "frame", "head", None)
    heads = P("fsdp", "frame", None, "head")
    in_specs = (rows, rows, rows, rows, rows, P("head", None), P(), P("frame"), P())
    out_specs = (heads, heads, heads, P("head", ("frame", "fsdp")))
    return jax.shard_map(
        per_device, mesh=mesh, in_specs=in_specs, out_specs=out_specs, check_vma=False
    )
```

```python
from functools import partial

import jax
import jax.numpy as jnp
from jax import lax
from jax.experimental import pallas as pl
from jax.experimental.pallas import tpu as pltpu
from jax.sharding import PartitionSpec as P

HD = 128
NEG = -1e30
NT = (((1,), (1,)), ((), ()))
NN = (((1,), (0,)), ((), ()))
TN = (((0,), (0,)), ((), ()))


def dot(lhs, rhs, dims):
    return lax.dot_general(lhs, rhs, dims, preferred_element_type=jnp.float32)


def attention_kernel(parts, scal, *refs):
    own_q, own_k, own_v = refs[:3]
    others, refs = parts - 1, refs[3:]
    kv_refs, q_refs, refs = refs[:others], refs[others : 2 * others], refs[2 * others :]
    o_ref, d_ref, prev_ref, next_ref, dq_ref, dk_ref, dv_ref, to_prev_ref, to_next_ref = refs[:9]
    q_all, k_all, v_all = refs[9:]
    _, frames, rows, _ = own_q.shape
    me = scal[0]
    inv_root = HD ** (-0.5)
    for s in range(parts):
        source = lax.rem(me + parts - s, parts)
        at = pl.ds(pl.multiple_of(source * rows, rows), rows)
        for f in range(frames):
            q_all[f, at] = own_q[0, f] if s == 0 else q_refs[s - 1][f]
            k_all[f + 1, at] = own_k[0, f] if s == 0 else kv_refs[s - 1][0, f]
            v_all[f + 1, at] = own_v[0, f] if s == 0 else kv_refs[s - 1][1, f]
        k_all[0, at] = prev_ref[0, s]
        v_all[0, at] = prev_ref[1, s]
        k_all[frames + 1, at] = next_ref[0, s]
        v_all[frames + 1, at] = next_ref[1, s]
    tokens = rows * parts
    row = lax.broadcasted_iota(jnp.int32, (tokens, tokens), 0)
    key_grads = [None] * (frames + 2)
    value_grads = [None] * (frames + 2)

    def put(grads, slot, term):
        grads[slot] = term if grads[slot] is None else grads[slot] + term

    for f in range(frames):
        q, d = q_all[f], d_ref[:, f].reshape(tokens, HD)
        prod = d.astype(jnp.float32) * o_ref[:, f].reshape(tokens, HD).astype(jnp.float32)
        delta = lax.dot_general(
            jnp.ones((8, HD), jnp.float32), prod, NT,
            precision=lax.Precision.HIGHEST, preferred_element_type=jnp.float32,
        )[0:1]
        scores = []
        for w in range(3):
            s = dot(k_all[f + w], q, NT) * inv_root
            if w != 1:
                s = jnp.where(row < scal[2 + 2 * f + w // 2], s, NEG)
            scores.append(s)
        top = jnp.max(jnp.maximum(jnp.maximum(scores[0], scores[1]), scores[2]), axis=0, keepdims=True)
        exps = [jnp.exp(s - top) for s in scores]
        total = jnp.sum(exps[0] + exps[1] + exps[2], axis=0, keepdims=True)
        inv_total = 1.0 / total
        dq = None
        for w in range(3):
            prob = exps[w] * inv_total
            put(value_grads, f + w, dot(prob.astype(jnp.bfloat16), d, NN))
            d_prob = dot(v_all[f + w], d, NT)
            d_score = (prob * (d_prob - delta)).astype(jnp.bfloat16)
            put(key_grads, f + w, dot(d_score, q, NN))
            term = dot(d_score, k_all[f + w], TN)
            dq = term if dq is None else dq + term
        dq_ref[f] = (dq * inv_root).astype(jnp.bfloat16)
    for f in range(frames):
        dk_ref[f] = key_grads[f + 1] * inv_root
        dv_ref[f] = value_grads[f + 1]
    to_prev_ref[0] = (key_grads[0] * inv_root).astype(jnp.bfloat16)
    to_prev_ref[1] = value_grads[0].astype(jnp.bfloat16)
    to_next_ref[0] = (key_grads[frames + 1] * inv_root).astype(jnp.bfloat16)
    to_next_ref[1] = value_grads[frames + 1].astype(jnp.bfloat16)


def attention(scal, head0, heads, local, kv, q_pieces, o, d, from_prev, from_next):
    parts = len(kv) + 1
    _, frames, rows, _ = local[0].shape
    tokens, width = parts * rows, heads * HD
    own = pl.BlockSpec((1, frames, rows, HD), lambda h, sc: (0, 0, 0, sc[1] + head0 + h))
    pack = pl.BlockSpec((2, frames, rows, HD), lambda h, sc: (0, 0, 0, head0 + h))
    q_spec = pl.BlockSpec((frames, rows, HD), lambda h, sc: (0, 0, h))
    dsp = pl.BlockSpec((parts, frames, rows, HD), lambda h, sc: (0, 0, 0, head0 + h))
    halo = pl.BlockSpec((2, parts, rows, HD), lambda h, sc: (0, 0, 0, head0 + h))
    out = pl.BlockSpec((frames, tokens, HD), lambda h, sc: (0, 0, h))
    edge = pl.BlockSpec((2, tokens, HD), lambda h, sc: (0, 0, h))
    full_shape, edge_shape = (frames, tokens, width), (2, tokens, width)
    pads = pltpu.VMEM((frames + 2, tokens, HD), jnp.bfloat16)
    flats = pltpu.VMEM((frames, tokens, HD), jnp.bfloat16)
    return pl.pallas_call(
        partial(attention_kernel, parts),
        grid_spec=pltpu.PrefetchScalarGridSpec(
            num_scalar_prefetch=1,
            grid=(heads,),
            in_specs=[own] * 3
            + [pack] * (parts - 1)
            + [q_spec] * (parts - 1)
            + [dsp, dsp, halo, halo],
            out_specs=[out] * 3 + [edge] * 2,
            scratch_shapes=[flats, pads, pads],
        ),
        out_shape=[
            jax.ShapeDtypeStruct(full_shape, jnp.bfloat16),
            jax.ShapeDtypeStruct(full_shape, jnp.float32),
            jax.ShapeDtypeStruct(full_shape, jnp.float32),
            jax.ShapeDtypeStruct(edge_shape, jnp.bfloat16),
            jax.ShapeDtypeStruct(edge_shape, jnp.bfloat16),
        ],
        compiler_params=pltpu.CompilerParams(vmem_limit_bytes=40 * 2**20),
        cost_estimate=pl.CostEstimate(
            flops=heads * frames * 3 * tokens * tokens * HD * 10,
            bytes_accessed=heads * HD * tokens * frames * 2 * 16,
            transcendentals=heads * frames * 3 * tokens * tokens,
        ),
        name="attention_backward",
    )(scal, *local, *kv, *q_pieces, o, d, from_prev, from_next)


def shifted(array, axis, step):
    count = lax.axis_size(axis)
    pairs = [(i, i + step) for i in range(count) if 0 <= i + step < count]
    return lax.ppermute(array, axis, pairs)


def rotated(array, axis, step):
    count = lax.axis_size(axis)
    return lax.ppermute(array, axis, [(i, (i + step) % count) for i in range(count)])


def after(array, event):
    return lax.optimization_barrier((array, event))


def flipped(array, axis, bit):
    return lax.ppermute(array, axis, [(i, i ^ bit) for i in range(lax.axis_size(axis))])


def weight_kernel(scale, table, near_ref, far_ref, g_near, g_far, out_ref):
    step = pl.program_id(0)

    @pl.when(step == 0)
    def _():
        out_ref[...] = jnp.zeros_like(out_ref)

    total = dot(near_ref[0], g_near[0], TN) + dot(far_ref[0], g_far[0], TN)
    out_ref[...] += total * scale


def weight_grad(table, near, far, gated, scale):
    count, rows, width = near.shape
    columns = gated.shape[2]
    side = pl.BlockSpec((1, rows, width), lambda j, tab: (j, 0, 0))
    return pl.pallas_call(
        partial(weight_kernel, scale),
        grid_spec=pltpu.PrefetchScalarGridSpec(
            num_scalar_prefetch=1,
            grid=(count,),
            in_specs=[
                side,
                side,
                pl.BlockSpec((1, rows, columns), lambda j, tab: (tab[0, j], 0, 0)),
                pl.BlockSpec((1, rows, columns), lambda j, tab: (tab[1, j], 0, 0)),
            ],
            out_specs=pl.BlockSpec((width, columns), lambda j, tab: (0, 0)),
        ),
        out_shape=jax.ShapeDtypeStruct((width, columns), jnp.float32),
        compiler_params=pltpu.CompilerParams(vmem_limit_bytes=40 * 2**20),
        cost_estimate=pl.CostEstimate(
            flops=4 * count * rows * width * columns,
            bytes_accessed=4 * count * rows * (width + columns) + 4 * width * columns,
            transcendentals=0,
        ),
        name="weight_gradient",
    )(table, near, far, gated, gated)


def project_kernel(g_ref, w_ref, out_ref, acc_ref):
    step = pl.program_id(0)
    term = dot(g_ref[0], w_ref[...], NT)

    @pl.when(step == 0)
    def _():
        acc_ref[...] = term

    @pl.when(step > 0)
    def _():
        acc_ref[...] += term

    @pl.when(step == pl.num_programs(0) - 1)
    def _():
        out_ref[...] = acc_ref[...].astype(out_ref.dtype)


def project(gated, weight):
    blocks, rows, columns = gated.shape
    width = weight.shape[0]
    if columns % 128:
        whole = gated.transpose(1, 0, 2).reshape(rows, blocks * columns)
        return dot(whole, weight, NT).astype(jnp.bfloat16)
    return pl.pallas_call(
        project_kernel,
        grid=(blocks,),
        in_specs=[
            pl.BlockSpec((1, rows, columns), lambda b: (b, 0, 0)),
            pl.BlockSpec((width, columns), lambda b: (0, b)),
        ],
        out_specs=pl.BlockSpec((rows, width), lambda b: (0, 0)),
        out_shape=jax.ShapeDtypeStruct((rows, width), jnp.bfloat16),
        scratch_shapes=[pltpu.VMEM((rows, width), jnp.float32)],
        compiler_params=pltpu.CompilerParams(vmem_limit_bytes=40 * 2**20),
        cost_estimate=pl.CostEstimate(
            flops=2 * rows * width * blocks * columns,
            bytes_accessed=2 * (rows + width) * blocks * columns + 2 * rows * width,
            transcendentals=0,
        ),
        name="project_gated",
    )(gated, weight)


def per_device(
    queries, key_rows, value_rows, saved_out, cotangent, out_weight, gate_table, levels, reach_flags
):
    _, frames, rows, model = queries.shape
    parts = lax.axis_size("head")
    me = lax.axis_index("head")
    width = model // parts
    heads = width // HD
    frames_all = frames * lax.axis_size("frame")
    tokens = rows * parts
    first_frame = lax.axis_index("frame") * frames
    tokens_all = lax.axis_size("fsdp") * frames_all * tokens
    blocks = lax.axis_size("frame") * lax.axis_size("fsdp")
    block = model // blocks
    def columns_for(array, step, start, size):
        target = lax.rem(me + step, parts)
        return lax.dynamic_slice_in_dim(array[0], target * width + start, size, axis=2)

    shifts = range(1, parts)
    shifts = range(1, parts)
    o_pieces = [rotated(columns_for(saved_out, s, 0, width), "head", s) for s in shifts]

    gain = jnp.concatenate(
        [lax.dynamic_slice_in_dim(gate_table, levels[f], 1, axis=0) for f in range(frames)], axis=0
    )
    gated = (cotangent[0].astype(jnp.float32) * gain[:, None, :]).astype(jnp.bfloat16)
    gated = gated.reshape(frames * rows, model)
    gated = jnp.stack([gated[:, b * block : (b + 1) * block] for b in range(blocks)])
    gathered = lax.all_gather(gated, "head", axis=1, tiled=True)

    kv_send = [
        jnp.stack([columns_for(a, s, 0, width) for a in (key_rows, value_rows)]) for s in shifts
    ]
    kv_send, gathered = after(kv_send, gathered)
    kv = [rotated(a, "head", s) for s, a in zip(shifts, kv_send)]

    o = jnp.zeros((parts, frames, rows, width), jnp.bfloat16)
    for s, piece in enumerate([columns_for(saved_out, 0, 0, width)] + o_pieces):
        o = lax.dynamic_update_slice_in_dim(o, piece[None], lax.rem(me + parts - s, parts), axis=0)

    levels_xy = [("fsdp", 1 << i) for i in range(lax.axis_size("fsdp").bit_length() - 1)]
    levels_xy += [("frame", 1 << i) for i in range(lax.axis_size("frame").bit_length() - 2, 0, -1)]

    def doubled(part, order):
        flips = [(0, 0)]
        for axis, bit in order:
            part = jnp.concatenate([part, flipped(part, axis, bit)], axis=0)
            flips += [(a ^ bit, b) if axis == "frame" else (a, b ^ bit) for a, b in flips]
        return part, flips

    o_rows = o.reshape(1, parts * frames * rows, width)
    half = o_rows.shape[1] // 2
    upper, flips = doubled(o_rows[:, :half], levels_xy)
    lower, lower_flips = doubled(o_rows[:, half:], levels_xy[::-1])
    near = jnp.stack(
        [
            jnp.concatenate([upper[i], lower[lower_flips.index(flip)]], axis=0)
            for i, flip in enumerate(flips)
        ]
    )
    far = flipped(near, "frame", 1)
    my_frame, my_video = lax.axis_index("frame"), lax.axis_index("fsdp")
    videos = lax.axis_size("fsdp")
    table = jnp.stack(
        [
            jnp.stack([(my_frame ^ (a ^ c)) * videos + (my_video ^ b) for a, b in flips])
            for c in range(2)
        ]
    ).astype(jnp.int32)

    gated_in = lax.all_to_all(
        gathered, ("frame", "fsdp"), split_axis=0, concat_axis=0, tiled=True
    )
    d_weight = weight_grad(table, near, far, gated_in, 1.0 / tokens_all)
    kv, d_weight = after(kv, d_weight)

    first = (heads + 1) // 2
    groups = [(0, first), (first, heads - first)]
    q_send = [
        [columns_for(queries, s, head0 * HD, count * HD) for s in shifts]
        for head0, count in groups
    ]
    q_send, gathered, kv = lax.optimization_barrier((q_send, gathered, kv))
    d = project(gathered, out_weight).reshape(parts, frames, rows, width)
    q_pieces = [[rotated(a, "head", s) for s, a in zip(shifts, sends)] for sends in q_send]

    ids = first_frame + jnp.arange(frames, dtype=jnp.int32)
    chosen = lax.dynamic_slice_in_dim(reach_flags, first_frame, frames, axis=0)
    inside = jnp.stack([ids > 0, ids < frames_all - 1], axis=1)
    limits = jnp.where(inside, jnp.where(chosen == 1, tokens, tokens // 2), 0).astype(jnp.int32)
    scal = jnp.concatenate([jnp.stack([me, me * heads]).astype(jnp.int32), limits.reshape(-1)])

    own = [columns_for(a, 0, 0, width) for a in (key_rows, value_rows)]

    def boundary(frame):
        return jnp.stack(
            [jnp.stack([own[t][frame]] + [p[t, frame] for p in kv]) for t in range(2)]
        )

    from_prev = shifted(boundary(frames - 1), "frame", 1)
    from_next = shifted(boundary(0), "frame", -1)
    local = (queries, key_rows, value_rows)
    results = []
    for (head0, count), q_group in zip(groups, q_pieces):
        if results:
            q_group, results[-1][0] = after(q_group, results[-1][0])
        dq, dk, dv, to_prev, to_next = attention(
            scal, head0, count, local, kv, q_group, o, d, from_prev, from_next
        )
        grad_next = shifted(to_prev, "frame", -1)
        grad_prev = shifted(to_next, "frame", 1)
        results.append([dq, dk, dv, grad_prev, grad_next])

    def combine(own_grad, t, grad_prev, grad_next):
        terms = [own_grad[f] for f in range(frames)]
        terms[0] = terms[0] + grad_prev[t].astype(jnp.float32)
        terms[frames - 1] = terms[frames - 1] + grad_next[t].astype(jnp.float32)
        return jnp.stack(terms).astype(jnp.bfloat16)

    d_queries = jnp.concatenate([r[0] for r in results], axis=2)[None]
    d_keys = jnp.concatenate([combine(r[1], 0, r[3], r[4]) for r in results], axis=2)[None]
    d_values = jnp.concatenate([combine(r[2], 1, r[3], r[4]) for r in results], axis=2)[None]
    return d_queries, d_keys, d_values, d_weight


def solution(mesh):
    rows = P("fsdp", "frame", "head", None)
    heads = P("fsdp", "frame", None, "head")
    in_specs = (rows, rows, rows, rows, rows, P("head", None), P(), P("frame"), P())
    out_specs = (heads, heads, heads, P("head", ("frame", "fsdp")))
    return jax.shard_map(
        per_device, mesh=mesh, in_specs=in_specs, out_specs=out_specs, check_vma=False
    )
```

```python
from functools import partial

import jax
import jax.numpy as jnp
from jax import lax
from jax.experimental import pallas as pl
from jax.experimental.pallas import tpu as pltpu
from jax.sharding import PartitionSpec as P

HD = 128
NEG = -1e30
NT = (((1,), (1,)), ((), ()))
NN = (((1,), (0,)), ((), ()))
TN = (((0,), (0,)), ((), ()))


def dot(lhs, rhs, dims):
    return lax.dot_general(lhs, rhs, dims, preferred_element_type=jnp.float32)


def attention_kernel(parts, scal, *refs):
    own_q, own_k, own_v = refs[:3]
    others, refs = parts - 1, refs[3:]
    kv_refs, q_refs, refs = refs[:others], refs[others : 2 * others], refs[2 * others :]
    o_ref, d_ref, prev_ref, next_ref, dq_ref, dk_ref, dv_ref, to_prev_ref, to_next_ref = refs[:9]
    q_all, k_all, v_all = refs[9:]
    _, frames, rows, _ = own_q.shape
    me = scal[0]
    inv_root = HD ** (-0.5)
    for s in range(parts):
        source = lax.rem(me + parts - s, parts)
        at = pl.ds(pl.multiple_of(source * rows, rows), rows)
        for f in range(frames):
            q_all[f, at] = own_q[0, f] if s == 0 else q_refs[s - 1][f]
            k_all[f + 1, at] = own_k[0, f] if s == 0 else kv_refs[s - 1][0, f]
            v_all[f + 1, at] = own_v[0, f] if s == 0 else kv_refs[s - 1][1, f]
        k_all[0, at] = prev_ref[0, s]
        v_all[0, at] = prev_ref[1, s]
        k_all[frames + 1, at] = next_ref[0, s]
        v_all[frames + 1, at] = next_ref[1, s]
    tokens = rows * parts
    row = lax.broadcasted_iota(jnp.int32, (tokens, tokens), 0)
    key_grads = [None] * (frames + 2)
    value_grads = [None] * (frames + 2)

    def put(grads, slot, term):
        grads[slot] = term if grads[slot] is None else grads[slot] + term

    for f in range(frames):
        q, d = q_all[f], d_ref[:, f].reshape(tokens, HD)
        prod = d.astype(jnp.float32) * o_ref[:, f].reshape(tokens, HD).astype(jnp.float32)
        delta = lax.dot_general(
            jnp.ones((8, HD), jnp.float32), prod, NT,
            precision=lax.Precision.HIGHEST, preferred_element_type=jnp.float32,
        )[0:1]
        scores = []
        for w in range(3):
            s = dot(k_all[f + w], q, NT) * inv_root
            if w != 1:
                s = jnp.where(row < scal[2 + 2 * f + w // 2], s, NEG)
            scores.append(s)
        top = jnp.max(jnp.maximum(jnp.maximum(scores[0], scores[1]), scores[2]), axis=0, keepdims=True)
        exps = [jnp.exp(s - top) for s in scores]
        total = jnp.sum(exps[0] + exps[1] + exps[2], axis=0, keepdims=True)
        inv_total = 1.0 / total
        dq = None
        for w in range(3):
            prob = exps[w] * inv_total
            put(value_grads, f + w, dot(prob.astype(jnp.bfloat16), d, NN))
            d_prob = dot(v_all[f + w], d, NT)
            d_score = (prob * (d_prob - delta)).astype(jnp.bfloat16)
            put(key_grads, f + w, dot(d_score, q, NN))
            term = dot(d_score, k_all[f + w], TN)
            dq = term if dq is None else dq + term
        dq_ref[f] = (dq * inv_root).astype(jnp.bfloat16)
    for f in range(frames):
        dk_ref[f] = key_grads[f + 1] * inv_root
        dv_ref[f] = value_grads[f + 1]
    to_prev_ref[0] = (key_grads[0] * inv_root).astype(jnp.bfloat16)
    to_prev_ref[1] = value_grads[0].astype(jnp.bfloat16)
    to_next_ref[0] = (key_grads[frames + 1] * inv_root).astype(jnp.bfloat16)
    to_next_ref[1] = value_grads[frames + 1].astype(jnp.bfloat16)


def attention(scal, head0, heads, local, kv, q_pieces, o, d, from_prev, from_next):
    parts = len(kv) + 1
    _, frames, rows, _ = local[0].shape
    tokens, width = parts * rows, heads * HD
    own = pl.BlockSpec((1, frames, rows, HD), lambda h, sc: (0, 0, 0, sc[1] + head0 + h))
    pack = pl.BlockSpec((2, frames, rows, HD), lambda h, sc: (0, 0, 0, head0 + h))
    q_spec = pl.BlockSpec((frames, rows, HD), lambda h, sc: (0, 0, h))
    dsp = pl.BlockSpec((parts, frames, rows, HD), lambda h, sc: (0, 0, 0, head0 + h))
    halo = pl.BlockSpec((2, parts, rows, HD), lambda h, sc: (0, 0, 0, head0 + h))
    out = pl.BlockSpec((frames, tokens, HD), lambda h, sc: (0, 0, h))
    edge = pl.BlockSpec((2, tokens, HD), lambda h, sc: (0, 0, h))
    full_shape, edge_shape = (frames, tokens, width), (2, tokens, width)
    pads = pltpu.VMEM((frames + 2, tokens, HD), jnp.bfloat16)
    flats = pltpu.VMEM((frames, tokens, HD), jnp.bfloat16)
    return pl.pallas_call(
        partial(attention_kernel, parts),
        grid_spec=pltpu.PrefetchScalarGridSpec(
            num_scalar_prefetch=1,
            grid=(heads,),
            in_specs=[own] * 3
            + [pack] * (parts - 1)
            + [q_spec] * (parts - 1)
            + [dsp, dsp, halo, halo],
            out_specs=[out] * 3 + [edge] * 2,
            scratch_shapes=[flats, pads, pads],
        ),
        out_shape=[
            jax.ShapeDtypeStruct(full_shape, jnp.bfloat16),
            jax.ShapeDtypeStruct(full_shape, jnp.float32),
            jax.ShapeDtypeStruct(full_shape, jnp.float32),
            jax.ShapeDtypeStruct(edge_shape, jnp.bfloat16),
            jax.ShapeDtypeStruct(edge_shape, jnp.bfloat16),
        ],
        compiler_params=pltpu.CompilerParams(vmem_limit_bytes=40 * 2**20),
        cost_estimate=pl.CostEstimate(
            flops=heads * frames * 3 * tokens * tokens * HD * 10,
            bytes_accessed=heads * HD * tokens * frames * 2 * 16,
            transcendentals=heads * frames * 3 * tokens * tokens,
        ),
        name="attention_backward",
    )(scal, *local, *kv, *q_pieces, o, d, from_prev, from_next)


def shifted(array, axis, step):
    count = lax.axis_size(axis)
    pairs = [(i, i + step) for i in range(count) if 0 <= i + step < count]
    return lax.ppermute(array, axis, pairs)


def rotated(array, axis, step):
    count = lax.axis_size(axis)
    return lax.ppermute(array, axis, [(i, (i + step) % count) for i in range(count)])


def after(array, event):
    return lax.optimization_barrier((array, event))


def flipped(array, axis, bit):
    return lax.ppermute(array, axis, [(i, i ^ bit) for i in range(lax.axis_size(axis))])


def weight_kernel(scale, table, near_ref, far_ref, g_near, g_far, out_ref):
    step = pl.program_id(0)

    @pl.when(step == 0)
    def _():
        out_ref[...] = jnp.zeros_like(out_ref)

    total = dot(near_ref[0], g_near[0], TN) + dot(far_ref[0], g_far[0], TN)
    out_ref[...] += total * scale


def weight_grad(table, near, far, gated, scale):
    count, rows, width = near.shape
    columns = gated.shape[2]
    side = pl.BlockSpec((1, rows, width), lambda j, tab: (j, 0, 0))
    return pl.pallas_call(
        partial(weight_kernel, scale),
        grid_spec=pltpu.PrefetchScalarGridSpec(
            num_scalar_prefetch=1,
            grid=(count,),
            in_specs=[
                side,
                side,
                pl.BlockSpec((1, rows, columns), lambda j, tab: (tab[0, j], 0, 0)),
                pl.BlockSpec((1, rows, columns), lambda j, tab: (tab[1, j], 0, 0)),
            ],
            out_specs=pl.BlockSpec((width, columns), lambda j, tab: (0, 0)),
        ),
        out_shape=jax.ShapeDtypeStruct((width, columns), jnp.float32),
        compiler_params=pltpu.CompilerParams(vmem_limit_bytes=40 * 2**20),
        cost_estimate=pl.CostEstimate(
            flops=4 * count * rows * width * columns,
            bytes_accessed=4 * count * rows * (width + columns) + 4 * width * columns,
            transcendentals=0,
        ),
        name="weight_gradient",
    )(table, near, far, gated, gated)


def project_kernel(g_ref, w_ref, out_ref, acc_ref):
    step = pl.program_id(0)
    term = dot(g_ref[0], w_ref[...], NT)

    @pl.when(step == 0)
    def _():
        acc_ref[...] = term

    @pl.when(step > 0)
    def _():
        acc_ref[...] += term

    @pl.when(step == pl.num_programs(0) - 1)
    def _():
        out_ref[...] = acc_ref[...].astype(out_ref.dtype)


def project(gated, weight):
    blocks, rows, columns = gated.shape
    width = weight.shape[0]
    if columns % 128:
        whole = gated.transpose(1, 0, 2).reshape(rows, blocks * columns)
        return dot(whole, weight, NT).astype(jnp.bfloat16)
    return pl.pallas_call(
        project_kernel,
        grid=(blocks,),
        in_specs=[
            pl.BlockSpec((1, rows, columns), lambda b: (b, 0, 0)),
            pl.BlockSpec((width, columns), lambda b: (0, b)),
        ],
        out_specs=pl.BlockSpec((rows, width), lambda b: (0, 0)),
        out_shape=jax.ShapeDtypeStruct((rows, width), jnp.bfloat16),
        scratch_shapes=[pltpu.VMEM((rows, width), jnp.float32)],
        compiler_params=pltpu.CompilerParams(vmem_limit_bytes=40 * 2**20),
        cost_estimate=pl.CostEstimate(
            flops=2 * rows * width * blocks * columns,
            bytes_accessed=2 * (rows + width) * blocks * columns + 2 * rows * width,
            transcendentals=0,
        ),
        name="project_gated",
    )(gated, weight)


def per_device(
    queries, key_rows, value_rows, saved_out, cotangent, out_weight, gate_table, levels, reach_flags
):
    _, frames, rows, model = queries.shape
    parts = lax.axis_size("head")
    me = lax.axis_index("head")
    width = model // parts
    heads = width // HD
    frames_all = frames * lax.axis_size("frame")
    tokens = rows * parts
    first_frame = lax.axis_index("frame") * frames
    tokens_all = lax.axis_size("fsdp") * frames_all * tokens
    blocks = lax.axis_size("frame") * lax.axis_size("fsdp")
    block = model // blocks
    def columns_for(array, step, start, size):
        target = lax.rem(me + step, parts)
        return lax.dynamic_slice_in_dim(array[0], target * width + start, size, axis=2)

    shifts = range(1, parts)
    shifts = range(1, parts)
    o_pieces = [rotated(columns_for(saved_out, s, 0, width), "head", s) for s in shifts]

    gain = jnp.concatenate(
        [lax.dynamic_slice_in_dim(gate_table, levels[f], 1, axis=0) for f in range(frames)], axis=0
    )
    gated = (cotangent[0].astype(jnp.float32) * gain[:, None, :]).astype(jnp.bfloat16)
    gated = gated.reshape(frames * rows, model)
    gated = jnp.stack([gated[:, b * block : (b + 1) * block] for b in range(blocks)])
    gathered = lax.all_gather(gated, "head", axis=1, tiled=True)

    kv_send = [
        jnp.stack([columns_for(a, s, 0, width) for a in (key_rows, value_rows)]) for s in shifts
    ]
    kv_send, gathered = after(kv_send, gathered)
    kv = [rotated(a, "head", s) for s, a in zip(shifts, kv_send)]

    o = jnp.zeros((parts, frames, rows, width), jnp.bfloat16)
    for s, piece in enumerate([columns_for(saved_out, 0, 0, width)] + o_pieces):
        o = lax.dynamic_update_slice_in_dim(o, piece[None], lax.rem(me + parts - s, parts), axis=0)

    levels_xy = [("fsdp", 1 << i) for i in range(lax.axis_size("fsdp").bit_length() - 1)]
    levels_xy += [("frame", 1 << i) for i in range(lax.axis_size("frame").bit_length() - 2, 0, -1)]

    def doubled(part, order):
        flips = [(0, 0)]
        for axis, bit in order:
            part = jnp.concatenate([part, flipped(part, axis, bit)], axis=0)
            flips += [(a ^ bit, b) if axis == "frame" else (a, b ^ bit) for a, b in flips]
        return part, flips

    o_rows = o.reshape(1, parts * frames * rows, width)
    half = o_rows.shape[1] // 2
    upper, flips = doubled(o_rows[:, :half], levels_xy)
    lower, lower_flips = doubled(o_rows[:, half:], levels_xy[::-1])
    near = jnp.stack(
        [
            jnp.concatenate([upper[i], lower[lower_flips.index(flip)]], axis=0)
            for i, flip in enumerate(flips)
        ]
    )
    far = flipped(near, "frame", 1)
    my_frame, my_video = lax.axis_index("frame"), lax.axis_index("fsdp")
    videos = lax.axis_size("fsdp")
    table = jnp.stack(
        [
            jnp.stack([(my_frame ^ (a ^ c)) * videos + (my_video ^ b) for a, b in flips])
            for c in range(2)
        ]
    ).astype(jnp.int32)

    gated_in = lax.all_to_all(
        gathered, ("frame", "fsdp"), split_axis=0, concat_axis=0, tiled=True
    )
    d_weight = weight_grad(table, near, far, gated_in, 1.0 / tokens_all)
    d = project(gathered, out_weight)

    first = (heads + 1) // 2
    groups = [(0, first), (first, heads - first)]
    q_send = [
        [columns_for(queries, s, head0 * HD, count * HD) for s in shifts]
        for head0, count in groups
    ]
    q_send, d = after(q_send, d)
    kv, d = after(kv, d)
    d = d.reshape(parts, frames, rows, width)
    q_pieces = [[rotated(a, "head", s) for s, a in zip(shifts, sends)] for sends in q_send]

    ids = first_frame + jnp.arange(frames, dtype=jnp.int32)
    chosen = lax.dynamic_slice_in_dim(reach_flags, first_frame, frames, axis=0)
    inside = jnp.stack([ids > 0, ids < frames_all - 1], axis=1)
    limits = jnp.where(inside, jnp.where(chosen == 1, tokens, tokens // 2), 0).astype(jnp.int32)
    scal = jnp.concatenate([jnp.stack([me, me * heads]).astype(jnp.int32), limits.reshape(-1)])

    own = [columns_for(a, 0, 0, width) for a in (key_rows, value_rows)]

    def boundary(frame):
        return jnp.stack(
            [jnp.stack([own[t][frame]] + [p[t, frame] for p in kv]) for t in range(2)]
        )

    from_prev = shifted(boundary(frames - 1), "frame", 1)
    from_next = shifted(boundary(0), "frame", -1)
    local = (queries, key_rows, value_rows)
    scal, d_weight = after(scal, d_weight)
    results = []
    for (head0, count), q_group in zip(groups, q_pieces):
        if results:
            q_group, results[-1][0] = after(q_group, results[-1][0])
        dq, dk, dv, to_prev, to_next = attention(
            scal, head0, count, local, kv, q_group, o, d, from_prev, from_next
        )
        grad_next = shifted(to_prev, "frame", -1)
        grad_prev = shifted(to_next, "frame", 1)
        results.append([dq, dk, dv, grad_prev, grad_next])

    def combine(own_grad, t, grad_prev, grad_next):
        terms = [own_grad[f] for f in range(frames)]
        terms[0] = terms[0] + grad_prev[t].astype(jnp.float32)
        terms[frames - 1] = terms[frames - 1] + grad_next[t].astype(jnp.float32)
        return jnp.stack(terms).astype(jnp.bfloat16)

    d_queries = jnp.concatenate([r[0] for r in results], axis=2)[None]
    d_keys = jnp.concatenate([combine(r[1], 0, r[3], r[4]) for r in results], axis=2)[None]
    d_values = jnp.concatenate([combine(r[2], 1, r[3], r[4]) for r in results], axis=2)[None]
    return d_queries, d_keys, d_values, d_weight


def solution(mesh):
    rows = P("fsdp", "frame", "head", None)
    heads = P("fsdp", "frame", None, "head")
    in_specs = (rows, rows, rows, rows, rows, P("head", None), P(), P("frame"), P())
    out_specs = (heads, heads, heads, P("head", ("frame", "fsdp")))
    return jax.shard_map(
        per_device, mesh=mesh, in_specs=in_specs, out_specs=out_specs, check_vma=False
    )
```

```python
from functools import partial

import jax
import jax.numpy as jnp
from jax import lax
from jax.experimental import pallas as pl
from jax.experimental.pallas import tpu as pltpu
from jax.sharding import PartitionSpec as P

HD = 128
NEG = -1e30
LOG2E = 1.4426950408889634
NT = (((1,), (1,)), ((), ()))
NN = (((1,), (0,)), ((), ()))
TN = (((0,), (0,)), ((), ()))


def dot(lhs, rhs, dims):
    return lax.dot_general(lhs, rhs, dims, preferred_element_type=jnp.float32)


def attention_kernel(parts, scal, *refs):
    own_q, own_k, own_v = refs[:3]
    others, refs = parts - 1, refs[3:]
    kv_refs, q_refs, refs = refs[:others], refs[others : 2 * others], refs[2 * others :]
    o_ref, d_ref, prev_ref, next_ref, dq_ref, dk_ref, dv_ref, to_prev_ref, to_next_ref = refs[:9]
    q_all, k_all, v_all = refs[9:]
    _, frames, rows, _ = own_q.shape
    me = scal[0]
    inv_root = HD ** (-0.5)
    for s in range(parts):
        source = lax.rem(me + parts - s, parts)
        at = pl.ds(pl.multiple_of(source * rows, rows), rows)
        for f in range(frames):
            q_all[f, at] = own_q[0, f] if s == 0 else q_refs[s - 1][f]
            k_all[f + 1, at] = own_k[0, f] if s == 0 else kv_refs[s - 1][0, f]
            v_all[f + 1, at] = own_v[0, f] if s == 0 else kv_refs[s - 1][1, f]
        k_all[0, at] = prev_ref[0, s]
        v_all[0, at] = prev_ref[1, s]
        k_all[frames + 1, at] = next_ref[0, s]
        v_all[frames + 1, at] = next_ref[1, s]
    tokens = rows * parts
    row = lax.broadcasted_iota(jnp.int32, (tokens, tokens), 0)
    key_grads = [None] * (frames + 2)
    value_grads = [None] * (frames + 2)

    def put(grads, slot, term):
        grads[slot] = term if grads[slot] is None else grads[slot] + term

    for f in range(frames):
        q, d = q_all[f], d_ref[:, f].reshape(tokens, HD)
        prod = d.astype(jnp.float32) * o_ref[:, f].reshape(tokens, HD).astype(jnp.float32)
        delta = lax.dot_general(
            jnp.ones((8, HD), jnp.float32), prod, NT,
            precision=lax.Precision.HIGHEST, preferred_element_type=jnp.float32,
        )[0:1]
        scores = []
        for w in range(3):
            s = dot(k_all[f + w], q, NT) * (inv_root * LOG2E)
            if w != 1:
                s = jnp.where(row < scal[2 + 2 * f + w // 2], s, NEG)
            scores.append(s)
        top = jnp.max(jnp.maximum(jnp.maximum(scores[0], scores[1]), scores[2]), axis=0, keepdims=True)
        exps = [jnp.exp2(s - top) for s in scores]
        total = jnp.sum(exps[0] + exps[1] + exps[2], axis=0, keepdims=True)
        inv_total = 1.0 / total
        dq = None
        for w in range(3):
            prob = exps[w] * inv_total
            put(value_grads, f + w, dot(prob.astype(jnp.bfloat16), d, NN))
            d_prob = dot(v_all[f + w], d, NT)
            d_score = (prob * (d_prob - delta)).astype(jnp.bfloat16)
            put(key_grads, f + w, dot(d_score, q, NN))
            term = dot(k_all[f + w], d_score, TN)
            dq = term if dq is None else dq + term
        dq_ref[f] = (dq.T * inv_root).astype(jnp.bfloat16)
    for f in range(frames):
        dk_ref[f] = key_grads[f + 1] * inv_root
        dv_ref[f] = value_grads[f + 1]
    to_prev_ref[0] = (key_grads[0] * inv_root).astype(jnp.bfloat16)
    to_prev_ref[1] = value_grads[0].astype(jnp.bfloat16)
    to_next_ref[0] = (key_grads[frames + 1] * inv_root).astype(jnp.bfloat16)
    to_next_ref[1] = value_grads[frames + 1].astype(jnp.bfloat16)


def attention(scal, head0, heads, local, kv, q_pieces, o, d, from_prev, from_next):
    parts = len(kv) + 1
    _, frames, rows, _ = local[0].shape
    tokens, width = parts * rows, heads * HD
    own = pl.BlockSpec((1, frames, rows, HD), lambda h, sc: (0, 0, 0, sc[1] + head0 + h))
    pack = pl.BlockSpec((2, frames, rows, HD), lambda h, sc: (0, 0, 0, head0 + h))
    q_spec = pl.BlockSpec((frames, rows, HD), lambda h, sc: (0, 0, h))
    dsp = pl.BlockSpec((parts, frames, rows, HD), lambda h, sc: (0, 0, 0, head0 + h))
    halo = pl.BlockSpec((2, parts, rows, HD), lambda h, sc: (0, 0, 0, head0 + h))
    out = pl.BlockSpec((frames, tokens, HD), lambda h, sc: (0, 0, h))
    edge = pl.BlockSpec((2, tokens, HD), lambda h, sc: (0, 0, h))
    full_shape, edge_shape = (frames, tokens, width), (2, tokens, width)
    pads = pltpu.VMEM((frames + 2, tokens, HD), jnp.bfloat16)
    flats = pltpu.VMEM((frames, tokens, HD), jnp.bfloat16)
    return pl.pallas_call(
        partial(attention_kernel, parts),
        grid_spec=pltpu.PrefetchScalarGridSpec(
            num_scalar_prefetch=1,
            grid=(heads,),
            in_specs=[own] * 3
            + [pack] * (parts - 1)
            + [q_spec] * (parts - 1)
            + [dsp, dsp, halo, halo],
            out_specs=[out] * 3 + [edge] * 2,
            scratch_shapes=[flats, pads, pads],
        ),
        out_shape=[
            jax.ShapeDtypeStruct(full_shape, jnp.bfloat16),
            jax.ShapeDtypeStruct(full_shape, jnp.float32),
            jax.ShapeDtypeStruct(full_shape, jnp.float32),
            jax.ShapeDtypeStruct(edge_shape, jnp.bfloat16),
            jax.ShapeDtypeStruct(edge_shape, jnp.bfloat16),
        ],
        compiler_params=pltpu.CompilerParams(vmem_limit_bytes=40 * 2**20),
        cost_estimate=pl.CostEstimate(
            flops=heads * frames * 3 * tokens * tokens * HD * 10,
            bytes_accessed=heads * HD * tokens * frames * 2 * 16,
            transcendentals=heads * frames * 3 * tokens * tokens,
        ),
        name="attention_backward",
    )(scal, *local, *kv, *q_pieces, o, d, from_prev, from_next)


def shifted(array, axis, step):
    count = lax.axis_size(axis)
    pairs = [(i, i + step) for i in range(count) if 0 <= i + step < count]
    return lax.ppermute(array, axis, pairs)


def rotated(array, axis, step):
    count = lax.axis_size(axis)
    return lax.ppermute(array, axis, [(i, (i + step) % count) for i in range(count)])


def after(array, event):
    return lax.optimization_barrier((array, event))


def flipped(array, axis, bit):
    return lax.ppermute(array, axis, [(i, i ^ bit) for i in range(lax.axis_size(axis))])


def weight_kernel(scale, table, near_ref, far_ref, g_near, g_far, out_ref):
    step = pl.program_id(0)

    @pl.when(step == 0)
    def _():
        out_ref[...] = jnp.zeros_like(out_ref)

    total = dot(near_ref[0], g_near[0], TN) + dot(far_ref[0], g_far[0], TN)
    out_ref[...] += total * scale


def weight_grad(table, near, far, gated, scale):
    count, rows, width = near.shape
    columns = gated.shape[2]
    side = pl.BlockSpec((1, rows, width), lambda j, tab: (j, 0, 0))
    return pl.pallas_call(
        partial(weight_kernel, scale),
        grid_spec=pltpu.PrefetchScalarGridSpec(
            num_scalar_prefetch=1,
            grid=(count,),
            in_specs=[
                side,
                side,
                pl.BlockSpec((1, rows, columns), lambda j, tab: (tab[0, j], 0, 0)),
                pl.BlockSpec((1, rows, columns), lambda j, tab: (tab[1, j], 0, 0)),
            ],
            out_specs=pl.BlockSpec((width, columns), lambda j, tab: (0, 0)),
        ),
        out_shape=jax.ShapeDtypeStruct((width, columns), jnp.float32),
        compiler_params=pltpu.CompilerParams(vmem_limit_bytes=40 * 2**20),
        cost_estimate=pl.CostEstimate(
            flops=4 * count * rows * width * columns,
            bytes_accessed=4 * count * rows * (width + columns) + 4 * width * columns,
            transcendentals=0,
        ),
        name="weight_gradient",
    )(table, near, far, gated, gated)


def gate_kernel(levels, cot_ref, table_ref, out_ref):
    _, frames, rows, _ = cot_ref.shape
    for f in range(frames):
        gain = table_ref[pl.ds(levels[f], 1), :]
        rounded = (cot_ref[0, f].astype(jnp.float32) * gain).astype(jnp.bfloat16)
        out_ref[0, f * rows : (f + 1) * rows] = rounded


def gate(cotangent, table, levels, blocks):
    _, frames, rows, model = cotangent.shape
    block = model // blocks
    if block % 128:
        gain = jnp.concatenate(
            [lax.dynamic_slice_in_dim(table, levels[f], 1, axis=0) for f in range(frames)], axis=0
        )
        gated = (cotangent[0].astype(jnp.float32) * gain[:, None, :]).astype(jnp.bfloat16)
        gated = gated.reshape(frames * rows, model)
        return jnp.stack([gated[:, b * block : (b + 1) * block] for b in range(blocks)])
    return pl.pallas_call(
        gate_kernel,
        grid_spec=pltpu.PrefetchScalarGridSpec(
            num_scalar_prefetch=1,
            grid=(blocks,),
            in_specs=[
                pl.BlockSpec((1, frames, rows, block), lambda b, lev: (0, 0, 0, b)),
                pl.BlockSpec((table.shape[0], block), lambda b, lev: (0, b)),
            ],
            out_specs=pl.BlockSpec((1, frames * rows, block), lambda b, lev: (b, 0, 0)),
        ),
        out_shape=jax.ShapeDtypeStruct((blocks, frames * rows, block), jnp.bfloat16),
        compiler_params=pltpu.CompilerParams(vmem_limit_bytes=40 * 2**20),
        name="gate_cotangent",
    )(levels, cotangent, table)


def project_kernel(g_ref, w_ref, out_ref, acc_ref):
    step = pl.program_id(0)
    term = dot(g_ref[0], w_ref[...], NT)

    @pl.when(step == 0)
    def _():
        acc_ref[...] = term

    @pl.when(step > 0)
    def _():
        acc_ref[...] += term

    @pl.when(step == pl.num_programs(0) - 1)
    def _():
        out_ref[...] = acc_ref[...].astype(out_ref.dtype)


def project(gated, weight):
    blocks, rows, columns = gated.shape
    width = weight.shape[0]
    if columns % 128:
        whole = gated.transpose(1, 0, 2).reshape(rows, blocks * columns)
        return dot(whole, weight, NT).astype(jnp.bfloat16)
    return pl.pallas_call(
        project_kernel,
        grid=(blocks,),
        in_specs=[
            pl.BlockSpec((1, rows, columns), lambda b: (b, 0, 0)),
            pl.BlockSpec((width, columns), lambda b: (0, b)),
        ],
        out_specs=pl.BlockSpec((rows, width), lambda b: (0, 0)),
        out_shape=jax.ShapeDtypeStruct((rows, width), jnp.bfloat16),
        scratch_shapes=[pltpu.VMEM((rows, width), jnp.float32)],
        compiler_params=pltpu.CompilerParams(vmem_limit_bytes=40 * 2**20),
        cost_estimate=pl.CostEstimate(
            flops=2 * rows * width * blocks * columns,
            bytes_accessed=2 * (rows + width) * blocks * columns + 2 * rows * width,
            transcendentals=0,
        ),
        name="project_gated",
    )(gated, weight)


def per_device(
    queries, key_rows, value_rows, saved_out, cotangent, out_weight, gate_table, levels, reach_flags
):
    _, frames, rows, model = queries.shape
    parts = lax.axis_size("head")
    me = lax.axis_index("head")
    width = model // parts
    heads = width // HD
    frames_all = frames * lax.axis_size("frame")
    tokens = rows * parts
    first_frame = lax.axis_index("frame") * frames
    tokens_all = lax.axis_size("fsdp") * frames_all * tokens
    blocks = lax.axis_size("frame") * lax.axis_size("fsdp")
    block = model // blocks
    def columns_for(array, step, start, size):
        target = lax.rem(me + step, parts)
        return lax.dynamic_slice_in_dim(array[0], target * width + start, size, axis=2)

    shifts = range(1, parts)
    shifts = range(1, parts)
    o_pieces = [rotated(columns_for(saved_out, s, 0, width), "head", s) for s in shifts]

    gated = gate(cotangent, gate_table, levels, blocks)
    gathered = lax.all_gather(gated, "head", axis=1, tiled=True)

    kv_send = [
        jnp.stack([columns_for(a, s, 0, width) for a in (key_rows, value_rows)]) for s in shifts
    ]
    kv_send, gathered = after(kv_send, gathered)
    kv = [rotated(a, "head", s) for s, a in zip(shifts, kv_send)]

    o = jnp.zeros((parts, frames, rows, width), jnp.bfloat16)
    for s, piece in enumerate([columns_for(saved_out, 0, 0, width)] + o_pieces):
        o = lax.dynamic_update_slice_in_dim(o, piece[None], lax.rem(me + parts - s, parts), axis=0)

    levels_xy = [("fsdp", 1 << i) for i in range(lax.axis_size("fsdp").bit_length() - 1)]
    levels_xy += [("frame", 1 << i) for i in range(lax.axis_size("frame").bit_length() - 2, 0, -1)]

    def doubled(part, order):
        flips = [(0, 0)]
        for axis, bit in order:
            part = jnp.concatenate([part, flipped(part, axis, bit)], axis=0)
            flips += [(a ^ bit, b) if axis == "frame" else (a, b ^ bit) for a, b in flips]
        return part, flips

    o_rows = o.reshape(1, parts * frames * rows, width)
    half = o_rows.shape[1] // 2
    upper, flips = doubled(o_rows[:, :half], levels_xy)
    lower, lower_flips = doubled(o_rows[:, half:], levels_xy[::-1])
    near = jnp.stack(
        [
            jnp.concatenate([upper[i], lower[lower_flips.index(flip)]], axis=0)
            for i, flip in enumerate(flips)
        ]
    )
    far = flipped(near, "frame", 1)
    my_frame, my_video = lax.axis_index("frame"), lax.axis_index("fsdp")
    videos = lax.axis_size("fsdp")
    table = jnp.stack(
        [
            jnp.stack([(my_frame ^ (a ^ c)) * videos + (my_video ^ b) for a, b in flips])
            for c in range(2)
        ]
    ).astype(jnp.int32)

    gated_in = lax.all_to_all(
        gathered, ("frame", "fsdp"), split_axis=0, concat_axis=0, tiled=True
    )
    d_weight = weight_grad(table, near, far, gated_in, 1.0 / tokens_all)
    d = project(gathered, out_weight)

    first = (heads + 1) // 2
    groups = [(0, first), (first, heads - first)]
    q_send = [
        [columns_for(queries, s, head0 * HD, count * HD) for s in shifts]
        for head0, count in groups
    ]
    q_send, d = after(q_send, d)
    kv, d = after(kv, d)
    d = d.reshape(parts, frames, rows, width)
    q_pieces = [[rotated(a, "head", s) for s, a in zip(shifts, sends)] for sends in q_send]

    ids = first_frame + jnp.arange(frames, dtype=jnp.int32)
    chosen = lax.dynamic_slice_in_dim(reach_flags, first_frame, frames, axis=0)
    inside = jnp.stack([ids > 0, ids < frames_all - 1], axis=1)
    limits = jnp.where(inside, jnp.where(chosen == 1, tokens, tokens // 2), 0).astype(jnp.int32)
    scal = jnp.concatenate([jnp.stack([me, me * heads]).astype(jnp.int32), limits.reshape(-1)])

    own = [columns_for(a, 0, 0, width) for a in (key_rows, value_rows)]

    def boundary(frame):
        return jnp.stack(
            [jnp.stack([own[t][frame]] + [p[t, frame] for p in kv]) for t in range(2)]
        )

    from_prev = shifted(boundary(frames - 1), "frame", 1)
    from_next = shifted(boundary(0), "frame", -1)
    local = (queries, key_rows, value_rows)
    scal, d_weight = after(scal, d_weight)
    results = []
    for (head0, count), q_group in zip(groups, q_pieces):
        if results:
            q_group, results[-1][0] = after(q_group, results[-1][0])
        dq, dk, dv, to_prev, to_next = attention(
            scal, head0, count, local, kv, q_group, o, d, from_prev, from_next
        )
        grad_next = shifted(to_prev, "frame", -1)
        grad_prev = shifted(to_next, "frame", 1)
        results.append([dq, dk, dv, grad_prev, grad_next])

    def combine(own_grad, t, grad_prev, grad_next):
        terms = [own_grad[f] for f in range(frames)]
        terms[0] = terms[0] + grad_prev[t].astype(jnp.float32)
        terms[frames - 1] = terms[frames - 1] + grad_next[t].astype(jnp.float32)
        return jnp.stack(terms).astype(jnp.bfloat16)

    d_queries = jnp.concatenate([r[0] for r in results], axis=2)[None]
    d_keys = jnp.concatenate([combine(r[1], 0, r[3], r[4]) for r in results], axis=2)[None]
    d_values = jnp.concatenate([combine(r[2], 1, r[3], r[4]) for r in results], axis=2)[None]
    return d_queries, d_keys, d_values, d_weight


def solution(mesh):
    rows = P("fsdp", "frame", "head", None)
    heads = P("fsdp", "frame", None, "head")
    in_specs = (rows, rows, rows, rows, rows, P("head", None), P(), P("frame"), P())
    out_specs = (heads, heads, heads, P("head", ("frame", "fsdp")))
    return jax.shard_map(
        per_device, mesh=mesh, in_specs=in_specs, out_specs=out_specs, check_vma=False
    )
```

```python
from functools import partial

import jax
import jax.numpy as jnp
from jax import lax
from jax.experimental import pallas as pl
from jax.experimental.pallas import tpu as pltpu
from jax.sharding import PartitionSpec as P

HD = 128
NEG = -1e30
LOG2E = 1.4426950408889634
NT = (((1,), (1,)), ((), ()))
NN = (((1,), (0,)), ((), ()))
TN = (((0,), (0,)), ((), ()))


def dot(lhs, rhs, dims):
    return lax.dot_general(lhs, rhs, dims, preferred_element_type=jnp.float32)


def attention_kernel(parts, scal, *refs):
    own_q, own_k, own_v = refs[:3]
    others, refs = parts - 1, refs[3:]
    kv_refs, q_refs, refs = refs[:others], refs[others : 2 * others], refs[2 * others :]
    o_ref, d_ref, prev_ref, next_ref, dq_ref, dk_ref, dv_ref, to_prev_ref, to_next_ref = refs[:9]
    q_all, k_all, v_all = refs[9:]
    _, frames, rows, _ = own_q.shape
    me = scal[0]
    inv_root = HD ** (-0.5)
    for s in range(parts):
        source = lax.rem(me + parts - s, parts)
        at = pl.ds(pl.multiple_of(source * rows, rows), rows)
        for f in range(frames):
            q_all[f, at] = own_q[0, f] if s == 0 else q_refs[s - 1][f]
            k_all[f + 1, at] = own_k[0, f] if s == 0 else kv_refs[s - 1][0, f]
            v_all[f + 1, at] = own_v[0, f] if s == 0 else kv_refs[s - 1][1, f]
        k_all[0, at] = prev_ref[0, s]
        v_all[0, at] = prev_ref[1, s]
        k_all[frames + 1, at] = next_ref[0, s]
        v_all[frames + 1, at] = next_ref[1, s]
    tokens = rows * parts
    half = tokens // 2
    key_grads = [None] * (frames + 2)
    value_grads = [None] * (frames + 2)

    def put(grads, slot, term):
        grads[slot] = term if grads[slot] is None else grads[slot] + term

    for f in range(frames):
        q, d = q_all[f], d_ref[:, f].reshape(tokens, HD)
        prod = d.astype(jnp.float32) * o_ref[:, f].reshape(tokens, HD).astype(jnp.float32)
        delta = lax.dot_general(
            jnp.ones((8, HD), jnp.float32), prod, NT,
            precision=lax.Precision.HIGHEST, preferred_element_type=jnp.float32,
        )[0:1]
        scores = []
        for w in range(3):
            s = dot(k_all[f + w], q, NT) * (inv_root * LOG2E)
            if w != 1:
                limit = scal[2 + 2 * f + w // 2]
                s = jnp.concatenate(
                    [
                        s[:half] + jnp.where(limit > 0, 0.0, NEG),
                        s[half:] + jnp.where(limit > half, 0.0, NEG),
                    ],
                    axis=0,
                )
            scores.append(s)
        top = jnp.max(jnp.maximum(jnp.maximum(scores[0], scores[1]), scores[2]), axis=0, keepdims=True)
        exps = [jnp.exp2(s - top) for s in scores]
        total = jnp.sum(exps[0] + exps[1] + exps[2], axis=0, keepdims=True)
        inv_total = 1.0 / total
        dq = None
        for w in range(3):
            prob = exps[w] * inv_total
            put(value_grads, f + w, dot(prob.astype(jnp.bfloat16), d, NN))
            d_prob = dot(v_all[f + w], d, NT)
            d_score = (prob * (d_prob - delta)).astype(jnp.bfloat16)
            put(key_grads, f + w, dot(d_score, q, NN))
            term = dot(k_all[f + w], d_score, TN)
            dq = term if dq is None else dq + term
        dq_ref[f] = (dq.T * inv_root).astype(jnp.bfloat16)
    for f in range(frames):
        dk_ref[f] = key_grads[f + 1] * inv_root
        dv_ref[f] = value_grads[f + 1]
    to_prev_ref[0] = (key_grads[0] * inv_root).astype(jnp.bfloat16)
    to_prev_ref[1] = value_grads[0].astype(jnp.bfloat16)
    to_next_ref[0] = (key_grads[frames + 1] * inv_root).astype(jnp.bfloat16)
    to_next_ref[1] = value_grads[frames + 1].astype(jnp.bfloat16)


def attention(scal, head0, heads, local, kv, q_pieces, o, d, from_prev, from_next):
    parts = len(kv) + 1
    _, frames, rows, _ = local[0].shape
    tokens, width = parts * rows, heads * HD
    own = pl.BlockSpec((1, frames, rows, HD), lambda h, sc: (0, 0, 0, sc[1] + head0 + h))
    pack = pl.BlockSpec((2, frames, rows, HD), lambda h, sc: (0, 0, 0, head0 + h))
    q_spec = pl.BlockSpec((frames, rows, HD), lambda h, sc: (0, 0, h))
    dsp = pl.BlockSpec((parts, frames, rows, HD), lambda h, sc: (0, 0, 0, head0 + h))
    halo = pl.BlockSpec((2, parts, rows, HD), lambda h, sc: (0, 0, 0, head0 + h))
    out = pl.BlockSpec((frames, tokens, HD), lambda h, sc: (0, 0, h))
    edge = pl.BlockSpec((2, tokens, HD), lambda h, sc: (0, 0, h))
    full_shape, edge_shape = (frames, tokens, width), (2, tokens, width)
    pads = pltpu.VMEM((frames + 2, tokens, HD), jnp.bfloat16)
    flats = pltpu.VMEM((frames, tokens, HD), jnp.bfloat16)
    return pl.pallas_call(
        partial(attention_kernel, parts),
        grid_spec=pltpu.PrefetchScalarGridSpec(
            num_scalar_prefetch=1,
            grid=(heads,),
            in_specs=[own] * 3
            + [pack] * (parts - 1)
            + [q_spec] * (parts - 1)
            + [dsp, dsp, halo, halo],
            out_specs=[out] * 3 + [edge] * 2,
            scratch_shapes=[flats, pads, pads],
        ),
        out_shape=[
            jax.ShapeDtypeStruct(full_shape, jnp.bfloat16),
            jax.ShapeDtypeStruct(full_shape, jnp.float32),
            jax.ShapeDtypeStruct(full_shape, jnp.float32),
            jax.ShapeDtypeStruct(edge_shape, jnp.bfloat16),
            jax.ShapeDtypeStruct(edge_shape, jnp.bfloat16),
        ],
        compiler_params=pltpu.CompilerParams(vmem_limit_bytes=40 * 2**20),
        cost_estimate=pl.CostEstimate(
            flops=heads * frames * 3 * tokens * tokens * HD * 10,
            bytes_accessed=heads * HD * tokens * frames * 2 * 16,
            transcendentals=heads * frames * 3 * tokens * tokens,
        ),
        name="attention_backward",
    )(scal, *local, *kv, *q_pieces, o, d, from_prev, from_next)


def shifted(array, axis, step):
    count = lax.axis_size(axis)
    pairs = [(i, i + step) for i in range(count) if 0 <= i + step < count]
    return lax.ppermute(array, axis, pairs)


def rotated(array, axis, step):
    count = lax.axis_size(axis)
    return lax.ppermute(array, axis, [(i, (i + step) % count) for i in range(count)])


def after(array, event):
    return lax.optimization_barrier((array, event))


def flipped(array, axis, bit):
    return lax.ppermute(array, axis, [(i, i ^ bit) for i in range(lax.axis_size(axis))])


def weight_kernel(scale, table, near_ref, far_ref, g_near, g_far, out_ref):
    step = pl.program_id(0)

    @pl.when(step == 0)
    def _():
        out_ref[...] = jnp.zeros_like(out_ref)

    total = dot(near_ref[0], g_near[0], TN) + dot(far_ref[0], g_far[0], TN)
    out_ref[...] += total * scale


def weight_grad(table, near, far, gated, scale):
    count, rows, width = near.shape
    columns = gated.shape[2]
    side = pl.BlockSpec((1, rows, width), lambda j, tab: (j, 0, 0))
    return pl.pallas_call(
        partial(weight_kernel, scale),
        grid_spec=pltpu.PrefetchScalarGridSpec(
            num_scalar_prefetch=1,
            grid=(count,),
            in_specs=[
                side,
                side,
                pl.BlockSpec((1, rows, columns), lambda j, tab: (tab[0, j], 0, 0)),
                pl.BlockSpec((1, rows, columns), lambda j, tab: (tab[1, j], 0, 0)),
            ],
            out_specs=pl.BlockSpec((width, columns), lambda j, tab: (0, 0)),
        ),
        out_shape=jax.ShapeDtypeStruct((width, columns), jnp.float32),
        compiler_params=pltpu.CompilerParams(vmem_limit_bytes=40 * 2**20),
        cost_estimate=pl.CostEstimate(
            flops=4 * count * rows * width * columns,
            bytes_accessed=4 * count * rows * (width + columns) + 4 * width * columns,
            transcendentals=0,
        ),
        name="weight_gradient",
    )(table, near, far, gated, gated)


def gate_kernel(levels, cot_ref, table_ref, out_ref):
    _, frames, rows, _ = cot_ref.shape
    for f in range(frames):
        gain = table_ref[pl.ds(levels[f], 1), :]
        rounded = (cot_ref[0, f].astype(jnp.float32) * gain).astype(jnp.bfloat16)
        out_ref[0, f * rows : (f + 1) * rows] = rounded


def gate(cotangent, table, levels, blocks):
    _, frames, rows, model = cotangent.shape
    block = model // blocks
    if block % 128:
        gain = jnp.concatenate(
            [lax.dynamic_slice_in_dim(table, levels[f], 1, axis=0) for f in range(frames)], axis=0
        )
        gated = (cotangent[0].astype(jnp.float32) * gain[:, None, :]).astype(jnp.bfloat16)
        gated = gated.reshape(frames * rows, model)
        return jnp.stack([gated[:, b * block : (b + 1) * block] for b in range(blocks)])
    return pl.pallas_call(
        gate_kernel,
        grid_spec=pltpu.PrefetchScalarGridSpec(
            num_scalar_prefetch=1,
            grid=(blocks,),
            in_specs=[
                pl.BlockSpec((1, frames, rows, block), lambda b, lev: (0, 0, 0, b)),
                pl.BlockSpec((table.shape[0], block), lambda b, lev: (0, b)),
            ],
            out_specs=pl.BlockSpec((1, frames * rows, block), lambda b, lev: (b, 0, 0)),
        ),
        out_shape=jax.ShapeDtypeStruct((blocks, frames * rows, block), jnp.bfloat16),
        compiler_params=pltpu.CompilerParams(vmem_limit_bytes=40 * 2**20),
        name="gate_cotangent",
    )(levels, cotangent, table)


def project_kernel(g_ref, w_ref, out_ref, acc_ref):
    step = pl.program_id(0)
    term = dot(g_ref[0], w_ref[...], NT)

    @pl.when(step == 0)
    def _():
        acc_ref[...] = term

    @pl.when(step > 0)
    def _():
        acc_ref[...] += term

    @pl.when(step == pl.num_programs(0) - 1)
    def _():
        out_ref[...] = acc_ref[...].astype(out_ref.dtype)


def project(gated, weight):
    blocks, rows, columns = gated.shape
    width = weight.shape[0]
    if columns % 128:
        whole = gated.transpose(1, 0, 2).reshape(rows, blocks * columns)
        return dot(whole, weight, NT).astype(jnp.bfloat16)
    return pl.pallas_call(
        project_kernel,
        grid=(blocks,),
        in_specs=[
            pl.BlockSpec((1, rows, columns), lambda b: (b, 0, 0)),
            pl.BlockSpec((width, columns), lambda b: (0, b)),
        ],
        out_specs=pl.BlockSpec((rows, width), lambda b: (0, 0)),
        out_shape=jax.ShapeDtypeStruct((rows, width), jnp.bfloat16),
        scratch_shapes=[pltpu.VMEM((rows, width), jnp.float32)],
        compiler_params=pltpu.CompilerParams(vmem_limit_bytes=40 * 2**20),
        cost_estimate=pl.CostEstimate(
            flops=2 * rows * width * blocks * columns,
            bytes_accessed=2 * (rows + width) * blocks * columns + 2 * rows * width,
            transcendentals=0,
        ),
        name="project_gated",
    )(gated, weight)


def per_device(
    queries, key_rows, value_rows, saved_out, cotangent, out_weight, gate_table, levels, reach_flags
):
    _, frames, rows, model = queries.shape
    parts = lax.axis_size("head")
    me = lax.axis_index("head")
    width = model // parts
    heads = width // HD
    frames_all = frames * lax.axis_size("frame")
    tokens = rows * parts
    first_frame = lax.axis_index("frame") * frames
    tokens_all = lax.axis_size("fsdp") * frames_all * tokens
    blocks = lax.axis_size("frame") * lax.axis_size("fsdp")
    block = model // blocks
    def columns_for(array, step, start, size):
        target = lax.rem(me + step, parts)
        return lax.dynamic_slice_in_dim(array[0], target * width + start, size, axis=2)

    shifts = range(1, parts)
    shifts = range(1, parts)
    o_pieces = [rotated(columns_for(saved_out, s, 0, width), "head", s) for s in shifts]

    gated = gate(cotangent, gate_table, levels, blocks)
    gathered = lax.all_gather(gated, "head", axis=1, tiled=True)

    kv_send = [
        jnp.stack([columns_for(a, s, 0, width) for a in (key_rows, value_rows)]) for s in shifts
    ]
    kv_send, gathered = after(kv_send, gathered)
    kv = [rotated(a, "head", s) for s, a in zip(shifts, kv_send)]

    o = jnp.zeros((parts, frames, rows, width), jnp.bfloat16)
    for s, piece in enumerate([columns_for(saved_out, 0, 0, width)] + o_pieces):
        o = lax.dynamic_update_slice_in_dim(o, piece[None], lax.rem(me + parts - s, parts), axis=0)

    levels_xy = [("fsdp", 1 << i) for i in range(lax.axis_size("fsdp").bit_length() - 1)]
    levels_xy += [("frame", 1 << i) for i in range(lax.axis_size("frame").bit_length() - 2, 0, -1)]

    def doubled(part, order):
        flips = [(0, 0)]
        for axis, bit in order:
            part = jnp.concatenate([part, flipped(part, axis, bit)], axis=0)
            flips += [(a ^ bit, b) if axis == "frame" else (a, b ^ bit) for a, b in flips]
        return part, flips

    o_rows = o.reshape(1, parts * frames * rows, width)
    half = o_rows.shape[1] // 2
    upper, flips = doubled(o_rows[:, :half], levels_xy)
    lower, lower_flips = doubled(o_rows[:, half:], levels_xy[::-1])
    near = jnp.stack(
        [
            jnp.concatenate([upper[i], lower[lower_flips.index(flip)]], axis=0)
            for i, flip in enumerate(flips)
        ]
    )
    far = flipped(near, "frame", 1)
    my_frame, my_video = lax.axis_index("frame"), lax.axis_index("fsdp")
    videos = lax.axis_size("fsdp")
    table = jnp.stack(
        [
            jnp.stack([(my_frame ^ (a ^ c)) * videos + (my_video ^ b) for a, b in flips])
            for c in range(2)
        ]
    ).astype(jnp.int32)

    gated_in = lax.all_to_all(
        gathered, ("frame", "fsdp"), split_axis=0, concat_axis=0, tiled=True
    )
    d_weight = weight_grad(table, near, far, gated_in, 1.0 / tokens_all)
    d = project(gathered, out_weight)

    first = (heads + 1) // 2
    groups = [(0, first), (first, heads - first)]
    q_send = [
        [columns_for(queries, s, head0 * HD, count * HD) for s in shifts]
        for head0, count in groups
    ]
    q_send, d = after(q_send, d)
    kv, d = after(kv, d)
    d = d.reshape(parts, frames, rows, width)
    q_pieces = [[rotated(a, "head", s) for s, a in zip(shifts, sends)] for sends in q_send]

    ids = first_frame + jnp.arange(frames, dtype=jnp.int32)
    chosen = lax.dynamic_slice_in_dim(reach_flags, first_frame, frames, axis=0)
    inside = jnp.stack([ids > 0, ids < frames_all - 1], axis=1)
    limits = jnp.where(inside, jnp.where(chosen == 1, tokens, tokens // 2), 0).astype(jnp.int32)
    scal = jnp.concatenate([jnp.stack([me, me * heads]).astype(jnp.int32), limits.reshape(-1)])

    own = [columns_for(a, 0, 0, width) for a in (key_rows, value_rows)]

    def boundary(frame):
        return jnp.stack(
            [jnp.stack([own[t][frame]] + [p[t, frame] for p in kv]) for t in range(2)]
        )

    from_prev = shifted(boundary(frames - 1), "frame", 1)
    from_next = shifted(boundary(0), "frame", -1)
    local = (queries, key_rows, value_rows)
    scal, d_weight = after(scal, d_weight)
    results = []
    for (head0, count), q_group in zip(groups, q_pieces):
        if results:
            q_group, results[-1][0] = after(q_group, results[-1][0])
        dq, dk, dv, to_prev, to_next = attention(
            scal, head0, count, local, kv, q_group, o, d, from_prev, from_next
        )
        grad_next = shifted(to_prev, "frame", -1)
        grad_prev = shifted(to_next, "frame", 1)
        results.append([dq, dk, dv, grad_prev, grad_next])

    def combine(own_grad, t, grad_prev, grad_next):
        terms = [own_grad[f] for f in range(frames)]
        terms[0] = terms[0] + grad_prev[t].astype(jnp.float32)
        terms[frames - 1] = terms[frames - 1] + grad_next[t].astype(jnp.float32)
        return jnp.stack(terms).astype(jnp.bfloat16)

    d_queries = jnp.concatenate([r[0] for r in results], axis=2)[None]
    d_keys = jnp.concatenate([combine(r[1], 0, r[3], r[4]) for r in results], axis=2)[None]
    d_values = jnp.concatenate([combine(r[2], 1, r[3], r[4]) for r in results], axis=2)[None]
    return d_queries, d_keys, d_values, d_weight


def solution(mesh):
    rows = P("fsdp", "frame", "head", None)
    heads = P("fsdp", "frame", None, "head")
    in_specs = (rows, rows, rows, rows, rows, P("head", None), P(), P("frame"), P())
    out_specs = (heads, heads, heads, P("head", ("frame", "fsdp")))
    return jax.shard_map(
        per_device, mesh=mesh, in_specs=in_specs, out_specs=out_specs, check_vma=False
    )
```

```python
from functools import partial

import jax
import jax.numpy as jnp
from jax import lax
from jax.experimental import pallas as pl
from jax.experimental.pallas import tpu as pltpu
from jax.sharding import PartitionSpec as P

HD = 128
NEG = -1e30
LOG2E = 1.4426950408889634
NT = (((1,), (1,)), ((), ()))
NN = (((1,), (0,)), ((), ()))
TN = (((0,), (0,)), ((), ()))


def dot(lhs, rhs, dims):
    return lax.dot_general(lhs, rhs, dims, preferred_element_type=jnp.float32)


def attention_kernel(parts, scal, *refs):
    own_q, own_k, own_v = refs[:3]
    others, refs = parts - 1, refs[3:]
    kv_refs, q_refs, refs = refs[:others], refs[others : 2 * others], refs[2 * others :]
    o_ref, d_ref, prev_ref, next_ref, dq_ref, dk_ref, dv_ref, to_prev_ref, to_next_ref = refs[:9]
    q_all, k_all, v_all = refs[9:]
    _, frames, rows, _ = own_q.shape
    me = scal[0]
    inv_root = HD ** (-0.5)
    for s in range(parts):
        source = lax.rem(me + parts - s, parts)
        at = pl.ds(pl.multiple_of(source * rows, rows), rows)
        for f in range(frames):
            q_all[f, at] = own_q[0, f] if s == 0 else q_refs[s - 1][f]
            k_all[f + 1, at] = own_k[0, f] if s == 0 else kv_refs[s - 1][0, f]
            v_all[f + 1, at] = own_v[0, f] if s == 0 else kv_refs[s - 1][1, f]
        k_all[0, at] = prev_ref[0, s]
        v_all[0, at] = prev_ref[1, s]
        k_all[frames + 1, at] = next_ref[0, s]
        v_all[frames + 1, at] = next_ref[1, s]
    tokens = rows * parts
    half = tokens // 2
    key_grads = [None] * (frames + 2)
    value_grads = [None] * (frames + 2)

    def put(grads, slot, term):
        grads[slot] = term if grads[slot] is None else grads[slot] + term

    for f in range(frames):
        q, d = q_all[f], d_ref[:, f].reshape(tokens, HD)
        prod = d.astype(jnp.float32) * o_ref[:, f].reshape(tokens, HD).astype(jnp.float32)
        delta = lax.dot_general(
            jnp.ones((8, HD), jnp.float32), prod, NT,
            precision=lax.Precision.HIGHEST, preferred_element_type=jnp.float32,
        )[0:1]
        scores = []
        for w in range(3):
            s = dot(k_all[f + w], q, NT) * (inv_root * LOG2E)
            if w != 1:
                limit = scal[2 + 2 * f + w // 2]
                s = jnp.concatenate(
                    [
                        s[:half] + jnp.where(limit > 0, 0.0, NEG),
                        s[half:] + jnp.where(limit > half, 0.0, NEG),
                    ],
                    axis=0,
                )
            scores.append(s)
        top = jnp.max(jnp.maximum(jnp.maximum(scores[0], scores[1]), scores[2]), axis=0, keepdims=True)
        exps = [jnp.exp2(s - top) for s in scores]
        total = jnp.sum(exps[0] + exps[1] + exps[2], axis=0, keepdims=True)
        inv_total = 1.0 / total
        dq = None
        for w in range(3):
            prob = exps[w] * inv_total
            put(value_grads, f + w, dot(prob.astype(jnp.bfloat16), d, NN))
            d_prob = dot(v_all[f + w], d, NT)
            d_score = (prob * (d_prob - delta)).astype(jnp.bfloat16)
            put(key_grads, f + w, dot(d_score, q, NN))
            term = dot(k_all[f + w], d_score, TN)
            dq = term if dq is None else dq + term
        dq_ref[f] = (dq.T * inv_root).astype(jnp.bfloat16)
    for f in range(frames):
        dk_ref[f] = key_grads[f + 1] * inv_root
        dv_ref[f] = value_grads[f + 1]
    to_prev_ref[0] = (key_grads[0] * inv_root).astype(jnp.bfloat16)
    to_prev_ref[1] = value_grads[0].astype(jnp.bfloat16)
    to_next_ref[0] = (key_grads[frames + 1] * inv_root).astype(jnp.bfloat16)
    to_next_ref[1] = value_grads[frames + 1].astype(jnp.bfloat16)


def attention(scal, head0, heads, local, kv, q_pieces, o, d, from_prev, from_next):
    parts = len(kv) + 1
    _, frames, rows, _ = local[0].shape
    tokens, width = parts * rows, heads * HD
    own = pl.BlockSpec((1, frames, rows, HD), lambda h, sc: (0, 0, 0, sc[1] + head0 + h))
    pack = pl.BlockSpec((2, frames, rows, HD), lambda h, sc: (0, 0, 0, head0 + h))
    q_spec = pl.BlockSpec((frames, rows, HD), lambda h, sc: (0, 0, h))
    dsp = pl.BlockSpec((parts, frames, rows, HD), lambda h, sc: (0, 0, 0, head0 + h))
    halo = pl.BlockSpec((2, parts, rows, HD), lambda h, sc: (0, 0, 0, head0 + h))
    out = pl.BlockSpec((frames, tokens, HD), lambda h, sc: (0, 0, h))
    edge = pl.BlockSpec((2, tokens, HD), lambda h, sc: (0, 0, h))
    full_shape, edge_shape = (frames, tokens, width), (2, tokens, width)
    pads = pltpu.VMEM((frames + 2, tokens, HD), jnp.bfloat16)
    flats = pltpu.VMEM((frames, tokens, HD), jnp.bfloat16)
    return pl.pallas_call(
        partial(attention_kernel, parts),
        grid_spec=pltpu.PrefetchScalarGridSpec(
            num_scalar_prefetch=1,
            grid=(heads,),
            in_specs=[own] * 3
            + [pack] * (parts - 1)
            + [q_spec] * (parts - 1)
            + [dsp, dsp, halo, halo],
            out_specs=[out] * 3 + [edge] * 2,
            scratch_shapes=[flats, pads, pads],
        ),
        out_shape=[
            jax.ShapeDtypeStruct(full_shape, jnp.bfloat16),
            jax.ShapeDtypeStruct(full_shape, jnp.float32),
            jax.ShapeDtypeStruct(full_shape, jnp.float32),
            jax.ShapeDtypeStruct(edge_shape, jnp.bfloat16),
            jax.ShapeDtypeStruct(edge_shape, jnp.bfloat16),
        ],
        compiler_params=pltpu.CompilerParams(vmem_limit_bytes=40 * 2**20),
        cost_estimate=pl.CostEstimate(
            flops=heads * frames * 3 * tokens * tokens * HD * 10,
            bytes_accessed=heads * HD * tokens * frames * 2 * 16,
            transcendentals=heads * frames * 3 * tokens * tokens,
        ),
        name="attention_backward",
    )(scal, *local, *kv, *q_pieces, o, d, from_prev, from_next)


def shifted(array, axis, step):
    count = lax.axis_size(axis)
    pairs = [(i, i + step) for i in range(count) if 0 <= i + step < count]
    return lax.ppermute(array, axis, pairs)


def rotated(array, axis, step):
    count = lax.axis_size(axis)
    return lax.ppermute(array, axis, [(i, (i + step) % count) for i in range(count)])


def after(array, event):
    return lax.optimization_barrier((array, event))


def flipped(array, axis, bit):
    return lax.ppermute(array, axis, [(i, i ^ bit) for i in range(lax.axis_size(axis))])


def weight_kernel(scale, table, near_ref, far_ref, g_near, g_far, out_ref, acc_ref):
    step = pl.program_id(0)
    total = dot(g_near[0], near_ref[0], TN) + dot(g_far[0], far_ref[0], TN)

    @pl.when(step == 0)
    def _():
        acc_ref[...] = total

    @pl.when(step > 0)
    def _():
        acc_ref[...] += total

    @pl.when(step == pl.num_programs(0) - 1)
    def _():
        out_ref[...] = acc_ref[...].T * scale


def weight_grad(table, near, far, gated, scale):
    count, rows, width = near.shape
    columns = gated.shape[2]
    side = pl.BlockSpec((1, rows, width), lambda j, tab: (j, 0, 0))
    return pl.pallas_call(
        partial(weight_kernel, scale),
        grid_spec=pltpu.PrefetchScalarGridSpec(
            num_scalar_prefetch=1,
            grid=(count,),
            in_specs=[
                side,
                side,
                pl.BlockSpec((1, rows, columns), lambda j, tab: (tab[0, j], 0, 0)),
                pl.BlockSpec((1, rows, columns), lambda j, tab: (tab[1, j], 0, 0)),
            ],
            out_specs=pl.BlockSpec((width, columns), lambda j, tab: (0, 0)),
            scratch_shapes=[pltpu.VMEM((columns, width), jnp.float32)],
        ),
        out_shape=jax.ShapeDtypeStruct((width, columns), jnp.float32),
        compiler_params=pltpu.CompilerParams(vmem_limit_bytes=40 * 2**20),
        cost_estimate=pl.CostEstimate(
            flops=4 * count * rows * width * columns,
            bytes_accessed=4 * count * rows * (width + columns) + 4 * width * columns,
            transcendentals=0,
        ),
        name="weight_gradient",
    )(table, near, far, gated, gated)


def gate_kernel(levels, cot_ref, table_ref, out_ref):
    _, frames, rows, _ = cot_ref.shape
    for f in range(frames):
        gain = table_ref[pl.ds(levels[f], 1), :]
        rounded = (cot_ref[0, f].astype(jnp.float32) * gain).astype(jnp.bfloat16)
        out_ref[0, f * rows : (f + 1) * rows] = rounded


def gate(cotangent, table, levels, blocks):
    _, frames, rows, model = cotangent.shape
    block = model // blocks
    if block % 128:
        gain = jnp.concatenate(
            [lax.dynamic_slice_in_dim(table, levels[f], 1, axis=0) for f in range(frames)], axis=0
        )
        gated = (cotangent[0].astype(jnp.float32) * gain[:, None, :]).astype(jnp.bfloat16)
        gated = gated.reshape(frames * rows, model)
        return jnp.stack([gated[:, b * block : (b + 1) * block] for b in range(blocks)])
    return pl.pallas_call(
        gate_kernel,
        grid_spec=pltpu.PrefetchScalarGridSpec(
            num_scalar_prefetch=1,
            grid=(blocks,),
            in_specs=[
                pl.BlockSpec((1, frames, rows, block), lambda b, lev: (0, 0, 0, b)),
                pl.BlockSpec((table.shape[0], block), lambda b, lev: (0, b)),
            ],
            out_specs=pl.BlockSpec((1, frames * rows, block), lambda b, lev: (b, 0, 0)),
        ),
        out_shape=jax.ShapeDtypeStruct((blocks, frames * rows, block), jnp.bfloat16),
        compiler_params=pltpu.CompilerParams(vmem_limit_bytes=40 * 2**20),
        name="gate_cotangent",
    )(levels, cotangent, table)


def project_kernel(g_ref, w_ref, out_ref, acc_ref):
    step = pl.program_id(0)
    term = dot(g_ref[0], w_ref[...], NT)

    @pl.when(step == 0)
    def _():
        acc_ref[...] = term

    @pl.when(step > 0)
    def _():
        acc_ref[...] += term

    @pl.when(step == pl.num_programs(0) - 1)
    def _():
        out_ref[...] = acc_ref[...].astype(out_ref.dtype)


def project(gated, weight):
    blocks, rows, columns = gated.shape
    width = weight.shape[0]
    if columns % 128:
        whole = gated.transpose(1, 0, 2).reshape(rows, blocks * columns)
        return dot(whole, weight, NT).astype(jnp.bfloat16)
    return pl.pallas_call(
        project_kernel,
        grid=(blocks,),
        in_specs=[
            pl.BlockSpec((1, rows, columns), lambda b: (b, 0, 0)),
            pl.BlockSpec((width, columns), lambda b: (0, b)),
        ],
        out_specs=pl.BlockSpec((rows, width), lambda b: (0, 0)),
        out_shape=jax.ShapeDtypeStruct((rows, width), jnp.bfloat16),
        scratch_shapes=[pltpu.VMEM((rows, width), jnp.float32)],
        compiler_params=pltpu.CompilerParams(vmem_limit_bytes=40 * 2**20),
        cost_estimate=pl.CostEstimate(
            flops=2 * rows * width * blocks * columns,
            bytes_accessed=2 * (rows + width) * blocks * columns + 2 * rows * width,
            transcendentals=0,
        ),
        name="project_gated",
    )(gated, weight)


def per_device(
    queries, key_rows, value_rows, saved_out, cotangent, out_weight, gate_table, levels, reach_flags
):
    _, frames, rows, model = queries.shape
    parts = lax.axis_size("head")
    me = lax.axis_index("head")
    width = model // parts
    heads = width // HD
    frames_all = frames * lax.axis_size("frame")
    tokens = rows * parts
    first_frame = lax.axis_index("frame") * frames
    tokens_all = lax.axis_size("fsdp") * frames_all * tokens
    blocks = lax.axis_size("frame") * lax.axis_size("fsdp")
    block = model // blocks
    def columns_for(array, step, start, size):
        target = lax.rem(me + step, parts)
        return lax.dynamic_slice_in_dim(array[0], target * width + start, size, axis=2)

    shifts = range(1, parts)
    shifts = range(1, parts)
    o_pieces = [rotated(columns_for(saved_out, s, 0, width), "head", s) for s in shifts]

    gated = gate(cotangent, gate_table, levels, blocks)
    gathered = lax.all_gather(gated, "head", axis=1, tiled=True)

    kv_send = [
        jnp.stack([columns_for(a, s, 0, width) for a in (key_rows, value_rows)]) for s in shifts
    ]
    kv_send, gathered = after(kv_send, gathered)
    kv = [rotated(a, "head", s) for s, a in zip(shifts, kv_send)]

    o = jnp.zeros((parts, frames, rows, width), jnp.bfloat16)
    for s, piece in enumerate([columns_for(saved_out, 0, 0, width)] + o_pieces):
        o = lax.dynamic_update_slice_in_dim(o, piece[None], lax.rem(me + parts - s, parts), axis=0)

    levels_xy = [("fsdp", 1 << i) for i in range(lax.axis_size("fsdp").bit_length() - 1)]
    levels_xy += [("frame", 1 << i) for i in range(lax.axis_size("frame").bit_length() - 2, 0, -1)]

    def doubled(part, order):
        flips = [(0, 0)]
        for axis, bit in order:
            part = jnp.concatenate([part, flipped(part, axis, bit)], axis=0)
            flips += [(a ^ bit, b) if axis == "frame" else (a, b ^ bit) for a, b in flips]
        return part, flips

    o_rows = o.reshape(1, parts * frames * rows, width)
    half = o_rows.shape[1] // 2
    upper, flips = doubled(o_rows[:, :half], levels_xy)
    lower, lower_flips = doubled(o_rows[:, half:], levels_xy[::-1])
    near = jnp.stack(
        [
            jnp.concatenate([upper[i], lower[lower_flips.index(flip)]], axis=0)
            for i, flip in enumerate(flips)
        ]
    )
    far = flipped(near, "frame", 1)
    my_frame, my_video = lax.axis_index("frame"), lax.axis_index("fsdp")
    videos = lax.axis_size("fsdp")
    table = jnp.stack(
        [
            jnp.stack([(my_frame ^ (a ^ c)) * videos + (my_video ^ b) for a, b in flips])
            for c in range(2)
        ]
    ).astype(jnp.int32)

    gated_in = lax.all_to_all(
        gathered, ("frame", "fsdp"), split_axis=0, concat_axis=0, tiled=True
    )
    d_weight = weight_grad(table, near, far, gated_in, 1.0 / tokens_all)
    d = project(gathered, out_weight)

    first = (heads + 1) // 2
    groups = [(0, first), (first, heads - first)]
    q_send = [
        [columns_for(queries, s, head0 * HD, count * HD) for s in shifts]
        for head0, count in groups
    ]
    q_send, d = after(q_send, d)
    kv, d = after(kv, d)
    d = d.reshape(parts, frames, rows, width)
    q_pieces = [[rotated(a, "head", s) for s, a in zip(shifts, sends)] for sends in q_send]

    ids = first_frame + jnp.arange(frames, dtype=jnp.int32)
    chosen = lax.dynamic_slice_in_dim(reach_flags, first_frame, frames, axis=0)
    inside = jnp.stack([ids > 0, ids < frames_all - 1], axis=1)
    limits = jnp.where(inside, jnp.where(chosen == 1, tokens, tokens // 2), 0).astype(jnp.int32)
    scal = jnp.concatenate([jnp.stack([me, me * heads]).astype(jnp.int32), limits.reshape(-1)])

    own = [columns_for(a, 0, 0, width) for a in (key_rows, value_rows)]

    def boundary(frame):
        return jnp.stack(
            [jnp.stack([own[t][frame]] + [p[t, frame] for p in kv]) for t in range(2)]
        )

    from_prev = shifted(boundary(frames - 1), "frame", 1)
    from_next = shifted(boundary(0), "frame", -1)
    local = (queries, key_rows, value_rows)
    scal, d_weight = after(scal, d_weight)
    results = []
    for (head0, count), q_group in zip(groups, q_pieces):
        if results:
            q_group, results[-1][0] = after(q_group, results[-1][0])
        dq, dk, dv, to_prev, to_next = attention(
            scal, head0, count, local, kv, q_group, o, d, from_prev, from_next
        )
        grad_next = shifted(to_prev, "frame", -1)
        grad_prev = shifted(to_next, "frame", 1)
        results.append([dq, dk, dv, grad_prev, grad_next])

    def combine(own_grad, t, grad_prev, grad_next):
        terms = [own_grad[f] for f in range(frames)]
        terms[0] = terms[0] + grad_prev[t].astype(jnp.float32)
        terms[frames - 1] = terms[frames - 1] + grad_next[t].astype(jnp.float32)
        return jnp.stack(terms).astype(jnp.bfloat16)

    d_queries = jnp.concatenate([r[0] for r in results], axis=2)[None]
    d_keys = jnp.concatenate([combine(r[1], 0, r[3], r[4]) for r in results], axis=2)[None]
    d_values = jnp.concatenate([combine(r[2], 1, r[3], r[4]) for r in results], axis=2)[None]
    return d_queries, d_keys, d_values, d_weight


def solution(mesh):
    rows = P("fsdp", "frame", "head", None)
    heads = P("fsdp", "frame", None, "head")
    in_specs = (rows, rows, rows, rows, rows, P("head", None), P(), P("frame"), P())
    out_specs = (heads, heads, heads, P("head", ("frame", "fsdp")))
    return jax.shard_map(
        per_device, mesh=mesh, in_specs=in_specs, out_specs=out_specs, check_vma=False
    )
```
